512 devices in a mesh: gx: 4 (over z_lo), gy: 16 (over x, z_hi), gz: 8 (over y, core).
Axes of the slice: x: 4, y: 4, z: 16 (z_hi: 4, z_lo: 4; z = z_hi * 4 + z_lo), core: 2. Of those that a mesh axis runs over, the one named last changes fastest.
Arguments:
- electric: float32 [3, 32, 256, 512], P(None, 'gz', 'gy', 'gx'), may hold values from -6 to 6
- magnetic: float32 [3, 32, 256, 512], P(None, 'gz', 'gy', 'gx'), may hold values from -6 to 6
- polar: float32 [3, 32, 256, 512], P(None, 'gz', 'gy', 'gx'), may hold values from -6 to 6
- current: float32 [3, 32, 256, 512], P(None, 'gz', 'gy', 'gx'), may hold values from -6 to 6
- material: int32 [32, 256, 512], P('gz', 'gy', 'gx'), may hold values from 0 to 2, as said below
- pml: int32 [32, 256, 512], P('gz', 'gy', 'gx'), may hold values from 0 to 3, as said below
Outputs:
- electric_out: float32 [3, 32, 256, 512], P(None, 'gz', 'gy', 'gx')
- magnetic_out: float32 [3, 32, 256, 512], P(None, 'gz', 'gy', 'gx')
- polar_out: float32 [3, 32, 256, 512], P(None, 'gz', 'gy', 'gx')
- current_out: float32 [3, 32, 256, 512], P(None, 'gz', 'gy', 'gx')
The draws below stay inside these ranges and needn't reach their ends.
Inputs may be any that keep to these rules, and one draw needn't show every extreme that they name: `material`: 0 vacuum, 1 dielectric, 2 Lorentz metal; outside the slab, the middle half of the z cells, every cell is vacuum. `pml`: level rises toward the grid's outer faces and is 3 on its outermost cells along x, y and z.
All inputs are finite; a program needn't handle non-finite values.
Results may differ from the reference program's by a relative error of at most 0.00002.
Values sent between devices are 32-bit elements; how exact they have to be, the bound alone decides.
No kernel may reach another device: no remote copies, remote signals or barrier semaphores. Data moves between devices by JAX's collectives and lax.ppermute only.
A program may use at most 64 MiB of HBM per device.

```python
import jax
import jax.numpy as jnp
from jax import lax

STEPS = 2
NX = 512
NY = 256
NZ = 32


def draw_material(key, part):
    key = jax.random.fold_in(key, 11)
    kinds = jax.random.randint(key, (NZ, NY, NX), 0, 3)
    depth = lax.broadcasted_iota(jnp.int32, (NZ, NY, NX), 0)
    slab = (depth >= NZ // 4) & (depth < NZ - NZ // 4)
    return jnp.where(slab, kinds, 0).astype(jnp.int32)


def layer_level(place, count, low, high):
    below = low - place
    above = place - (count - 1 - high)
    level_low = jnp.where(below > 0, (3 * below + low - 1) // low, 0)
    level_high = jnp.where(above > 0, (3 * above + high - 1) // high, 0)
    return jnp.maximum(level_low, level_high)


def draw_pml(key, part):
    key = jax.random.fold_in(key, 23)
    key_side, key_top = jax.random.split(key)
    sides = jax.random.randint(key_side, (4,), 2, 6)
    tops = jax.random.randint(key_top, (2,), 1, max(2, NZ // 4) + 1)
    shape = (NZ, NY, NX)
    along_z = lax.broadcasted_iota(jnp.int32, shape, 0)
    along_y = lax.broadcasted_iota(jnp.int32, shape, 1)
    along_x = lax.broadcasted_iota(jnp.int32, shape, 2)
    level = layer_level(along_x, NX, sides[0], sides[1])
    level = jnp.maximum(level, layer_level(along_y, NY, sides[2], sides[3]))
    level = jnp.maximum(level, layer_level(along_z, NZ, tops[0], tops[1]))
    return level.astype(jnp.int32)


def level_of(own_key, extent, pieces, low, top_value):
    gain = 1.0
    for dim, blocks in pieces:
        draws = jax.random.uniform(jax.random.fold_in(jax.random.fold_in(own_key, 6), dim), (blocks,), jnp.float32, low / len(pieces), top_value / len(pieces))
        gain = gain * jnp.repeat(jnp.exp(draws), extent[dim] // blocks).reshape((-1,) + (1,) * (len(extent) - 1 - dim))
    return gain


def centred(stream_key, shape, scale, most, cuts=(), held_as=jnp.bfloat16):
    gain = level_of(stream_key, shape, cuts, -0.22, 0.18) if cuts else 1.0
    array = jax.random.normal(stream_key, shape, jnp.float32) * scale * gain
    return jnp.minimum(jnp.maximum(array, -most), most).astype(held_as)


def setup_inputs(seed: int = 0) -> dict:
    streams_of = jax.random.split(jax.random.key(seed), 7)
    return {
        "electric": centred(streams_of[0], (3, NZ, NY, NX), 1.0, 6.0, ((1, 8), (2, 16), (3, 4)), jnp.float32),
        "magnetic": centred(streams_of[1], (3, NZ, NY, NX), 1.0, 6.0, ((1, 8), (2, 16), (3, 4)), jnp.float32),
        "polar": centred(streams_of[2], (3, NZ, NY, NX), 1.0, 6.0, ((1, 8), (2, 16), (3, 4)), jnp.float32),
        "current": centred(streams_of[3], (3, NZ, NY, NX), 1.0, 6.0, ((1, 8), (2, 16), (3, 4)), jnp.float32),
        "material": draw_material(jax.random.fold_in(streams_of[6], 71), 0),
        "pml": draw_pml(jax.random.fold_in(streams_of[6], 71), 0),
    }


time_step = 0.5
damping = 0.2
omega_sq = 1.0
strength = 3.0


def material_terms(code):
    metal = (code > 8.5).astype(jnp.float32)
    dielec = ((code > 4.5) & (code < 8.5)).astype(jnp.float32)
    inside = (code > 0.5).astype(jnp.float32)
    level = code - 1.0 - 4.0 * (2.0 * metal + dielec)
    sigma = jnp.where(level > 2.5, 1.0, jnp.where(level > 1.5, 0.4, jnp.where(level > 0.5, 0.1, 0.0))).astype(jnp.float32)
    permit = 1.0 + 0.5 * metal + 1.25 * dielec
    return sigma, permit, metal, inside


def curl_forward(field):
    lead = field[:, :-1, :-1, :-1]
    d_z = field[:, 1:, :-1, :-1] - lead
    d_y = field[:, :-1, 1:, :-1] - lead
    d_x = field[:, :-1, :-1, 1:] - lead
    return jnp.stack([d_y[2] - d_z[1], d_z[0] - d_x[2], d_x[1] - d_y[0]])


def curl_backward(field):
    last = field[:, 1:, 1:, 1:]
    d_z = last - field[:, :-1, 1:, 1:]
    d_y = last - field[:, 1:, :-1, 1:]
    d_x = last - field[:, 1:, 1:, :-1]
    return jnp.stack([d_y[2] - d_z[1], d_z[0] - d_x[2], d_x[1] - d_y[0]])


def interior(field):
    return field[:, 1:-1, 1:-1, 1:-1]


def leapfrog(electric, magnetic, polar, current, code):
    sigma, permit, metal, inside = material_terms(code)
    loss_h = 0.5 * time_step * sigma[:, :-1, :-1, :-1]
    magnetic_new = ((1.0 - loss_h) * magnetic[:, :-1, :-1, :-1] - time_step * curl_forward(electric)) / (1.0 + loss_h)
    magnetic_new = magnetic_new * inside[:, :-1, :-1, :-1]
    e_core = interior(electric)
    metal_core = interior(metal)
    current_new = ((1.0 - 0.5 * damping * time_step) * current + time_step * omega_sq * (strength * metal_core * e_core - polar)) / (1.0 + 0.5 * damping * time_step)
    polar_new = polar + time_step * current_new
    loss_e = 0.5 * time_step * interior(sigma)
    permit_core = interior(permit)
    electric_new = ((permit_core - loss_e) * e_core + time_step * (curl_backward(magnetic_new) - metal_core * current_new)) / (permit_core + loss_e)
    electric_new = electric_new * interior(inside)
    return electric_new, magnetic_new, polar_new, current_new


def reference(electric, magnetic, polar, current, material, pml):
    code = (1 + 4 * material + pml).astype(jnp.float32)[None]
    widths = ((0, 0), (1, 1), (1, 1), (1, 1))
    for step in range(STEPS):
        electric, magnetic_new, polar, current = leapfrog(jnp.pad(electric, widths), jnp.pad(magnetic, widths), polar, current, jnp.pad(code, widths))
        magnetic = magnetic_new[:, 1:, 1:, 1:]
    return electric, magnetic, polar, current
```

```python
import jax
import jax.numpy as jnp
from jax import lax
from jax.sharding import PartitionSpec as P

time_step = 0.5
damping = 0.2
omega_sq = 1.0
strength = 3.0

DIMS = (("gy", 2), ("gx", 3), ("gz", 1))


def widened(low, high, axis, dim):
    peers = lax.axis_size(axis)
    up = [(i, i + 1) for i in range(peers - 1)]
    down = [(i + 1, i) for i in range(peers - 1)]
    after = lax.ppermute(high, axis, down)
    before = lax.ppermute(low, axis, up)
    return before, after


def ends(array, dim, low, high):
    n = array.shape[dim]
    return (
        lax.slice_in_dim(array, n - low, n, axis=dim),
        lax.slice_in_dim(array, 0, high, axis=dim),
    )


def exchange(groups):
    arrays = [g[0] for g in groups]
    widths = [(g[1], g[2]) for g in groups]
    for axis, dim in DIMS:
        cuts = [ends(a, dim, lo, hi) for a, (lo, hi) in zip(arrays, widths)]
        lows = [c[0] for c in cuts]
        highs = [c[1] for c in cuts]
        flat_low = jnp.concatenate([c.reshape(-1) for c in lows])
        flat_high = jnp.concatenate([c.reshape(-1) for c in highs])
        sizes = flat_low.size, flat_high.size

        def lined(flat):
            return jnp.pad(flat, (0, -flat.size % 1024)).reshape(-1, 128)

        before, after = widened(lined(flat_low), lined(flat_high), axis, dim)
        before, after = before.reshape(-1), after.reshape(-1)
        out, at_b, at_a = [], 0, 0
        for a, lo, hi in zip(arrays, lows, highs):
            b = before[at_b : at_b + lo.size].reshape(lo.shape)
            c = after[at_a : at_a + hi.size].reshape(hi.shape)
            at_b, at_a = at_b + lo.size, at_a + hi.size
            out.append(jnp.concatenate([b, a, c], axis=dim))
        arrays = out
    return arrays


def cut(array, low, high):
    _, z, y, x = array.shape
    return array[:, low : z - high, low : y - high, low : x - high]


def material_terms(code):
    metal = (code > 8.5).astype(jnp.float32)
    dielec = ((code > 4.5) & (code < 8.5)).astype(jnp.float32)
    inside = (code > 0.5).astype(jnp.float32)
    level = code - 1.0 - 4.0 * (2.0 * metal + dielec)
    sigma = jnp.where(
        level > 2.5, 1.0, jnp.where(level > 1.5, 0.4, jnp.where(level > 0.5, 0.1, 0.0))
    ).astype(jnp.float32)
    permit = 1.0 + 0.5 * metal + 1.25 * dielec
    return sigma, permit, metal, inside


def curl(d_x, d_y, d_z):
    return jnp.stack([d_y[2] - d_z[1], d_z[0] - d_x[2], d_x[1] - d_y[0]])


def forward(field):
    lead = field[:, :-1, :-1, :-1]
    return curl(
        field[:, :-1, :-1, 1:] - lead,
        field[:, :-1, 1:, :-1] - lead,
        field[:, 1:, :-1, :-1] - lead,
    )


def backward(field):
    last = field[:, 1:, 1:, 1:]
    return curl(
        last - field[:, 1:, 1:, :-1],
        last - field[:, 1:, :-1, 1:],
        last - field[:, :-1, 1:, 1:],
    )


DECAY = 1.0 + 0.5 * damping * time_step


def magnetic_step(magnetic, electric, code):
    sigma, _, _, inside = material_terms(code)
    loss = 0.5 * time_step * sigma
    return inside * ((1.0 - loss) * magnetic - time_step * forward(electric)) / (1.0 + loss)


def electric_step(electric, magnetic, current, code):
    sigma, permit, metal, inside = material_terms(code)
    loss = 0.5 * time_step * sigma
    return (
        inside
        * ((permit - loss) * electric + time_step * (backward(magnetic) - metal * current))
        / (permit + loss)
    )


def on_device(electric, magnetic, polar, current, material, pml):
    code = (1 + 4 * material + pml).astype(jnp.float32)[None]
    keep = ((1.0 - 0.5 * damping * time_step) * current - time_step * omega_sq * polar) / DECAY
    gain = time_step * omega_sq * strength / DECAY

    e0, h0, c0, q0 = exchange([(electric, 2, 2), (magnetic, 2, 1), (code, 2, 1), (keep, 1, 1)])

    h1 = magnetic_step(h0, e0, c0)
    c1 = cut(c0, 1, 0)
    metal = (c1 > 8.5).astype(jnp.float32)
    e0_mid = cut(e0, 1, 1)
    j1 = q0 + gain * metal * e0_mid
    e1 = electric_step(e0_mid, h1, j1, c1)
    current1 = cut(j1, 1, 1)
    polar1 = polar + time_step * current1

    h2 = magnetic_step(cut(h1, 1, 1), e1, cut(c1, 0, 1))
    c2 = cut(c1, 1, 1)
    metal = (c2 > 8.5).astype(jnp.float32)
    e1_mid = cut(e1, 1, 1)
    current2 = (
        (1.0 - 0.5 * damping * time_step) * current1
        + time_step * omega_sq * (strength * metal * e1_mid - polar1)
    ) / DECAY
    polar2 = polar1 + time_step * current2
    e2 = electric_step(e1_mid, h2, current2, c2)
    return e2, cut(h2, 1, 0), polar2, current2


def solution(mesh):
    fields = P(None, "gz", "gy", "gx")
    cells = P("gz", "gy", "gx")
    return jax.shard_map(
        on_device,
        mesh=mesh,
        in_specs=(fields, fields, fields, fields, cells, cells),
        out_specs=(fields, fields, fields, fields),
        check_vma=False,
    )
```

```python
import functools

import jax
import jax.numpy as jnp
from jax import lax
from jax.experimental import pallas as pl
from jax.experimental.pallas import tpu as pltpu
from jax.sharding import PartitionSpec as P

time_step = 0.5
damping = 0.2
omega_sq = 1.0
strength = 3.0

DECAY = 1.0 + 0.5 * damping * time_step
HOLD = (1.0 - 0.5 * damping * time_step) / DECAY
PULL = time_step * omega_sq / DECAY
GAIN = PULL * strength

EX, EY, EZ, HX, HY, HZ, QX, QY, QZ, CODE = range(10)
EVERY = tuple(range(10))

Y_UP = [(c, 14) for c in (EX, EY, EZ, HX, HZ, CODE)] + [(c, 15) for c in EVERY]
Y_DOWN = [(c, 0) for c in (EX, EY, EZ, HX, HY, HZ, QX, QZ, CODE)] + [(EX, 1), (EZ, 1)]
Z_UP = [(c, 2) for c in (EX, EY, EZ, HX, HY, CODE)] + [(c, 3) for c in EVERY]
Z_DOWN = [(c, 0) for c in (EX, EY, EZ, HX, HY, HZ, QX, QY, CODE)] + [(EX, 1), (EY, 1)]

ROWS = 24
PLANES = range(-2, 6)
SPAN = 32


def up_of(n):
    return [(i, i + 1) for i in range(n - 1)]


def down_of(n):
    return [(i + 1, i) for i in range(n - 1)]


def code_of(material, pml):
    return (1 + 4 * material + pml).astype(jnp.float32)


def y_faces(e, h, p, j, material, pml, up, down):
    def face(c, row):
        if c < HX:
            return e[c, :, row, :]
        if c < QX:
            return h[c - HX, :, row, :]
        if c < CODE:
            return HOLD * j[c - QX, :, row, :] - PULL * p[c - QX, :, row, :]
        return code_of(material[:, row, :], pml[:, row, :])

    down[...] = jnp.zeros_like(down)
    for ref, faces in ((up, Y_UP), (down, Y_DOWN)):
        for i, (c, row) in enumerate(faces):
            ref[4 * i : 4 * i + 4, :] = face(c, row)


def z_faces(e, h, p, j, material, pml, before, after, wide, up, down):
    for z in range(4):
        for c in EVERY:
            if c < HX:
                own = e[c, z]
            elif c < QX:
                own = h[c - HX, z]
            elif c < CODE:
                own = HOLD * j[c - QX, z] - PULL * p[c - QX, z]
            else:
                own = code_of(material[z], pml[z])
            wide[z, c, 0:16, :] = own
            wide[z, c, 16:24, :] = jnp.zeros((8, 128), jnp.float32)
        for i, (c, row) in enumerate(Y_UP):
            wide[z, c, row + 8 : row + 9, :] = before[4 * i + z : 4 * i + z + 1, :]
        for i, (c, row) in enumerate(Y_DOWN):
            wide[z, c, row + 16 : row + 17, :] = after[4 * i + z : 4 * i + z + 1, :]
    for i, (c, z) in enumerate(Z_UP):
        up[i] = wide[z, c]
    for i, (c, z) in enumerate(Z_DOWN):
        down[i] = wide[z, c]


def planes_of(flags, wide, before, after):
    first = flags[0] == 0
    last = flags[1] == 0

    def plane(c, z):
        if 0 <= z < 4:
            return wide[z, c]
        if z < 0:
            if (c, z + 4) not in Z_UP:
                return None
            got = before[Z_UP.index((c, z + 4))]
            return jnp.where(first, 0.0, got)
        if (c, z - 4) not in Z_DOWN:
            return None
        got = after[Z_DOWN.index((c, z - 4))]
        return jnp.where(last, 0.0, got)

    return plane


def lanes():
    return lax.broadcasted_iota(jnp.int32, (ROWS, 128), 1)


def roll(array, shift, axis):
    shift = shift % array.shape[axis]
    return pltpu.roll(array, shift, axis) if shift else array


def x_edges(flags, wide, before, after, edges):
    plane = planes_of(flags, wide, before, after)
    lane = lanes()
    for g in range(3):
        total = jnp.zeros((ROWS, 128), jnp.float32)
        for c in range(4 * g, min(4 * g + 4, 10)):
            for z in PLANES:
                value = plane(c, z)
                if value is None:
                    continue
                at = SPAN * (c - 4 * g) + 4 * (z + 2)
                moved = roll(value, at - 126, 1)
                total = jnp.where((lane >= at) & (lane < at + 4), moved, total)
        edges[g] = total


def factors(code):
    metal = code > 8.5
    dielec = (code > 4.5) & (code < 8.5)
    inside = code > 0.5
    level = code - jnp.where(metal, 9.0, jnp.where(dielec, 5.0, 1.0))
    loss = jnp.where(level > 2.5, 0.25, jnp.where(level > 1.5, 0.1, jnp.where(level > 0.5, 0.025, 0.0)))
    permit = jnp.where(metal, 1.5, jnp.where(dielec, 2.25, 1.0))
    over_h = jnp.where(inside, 1.0 / (1.0 + loss), 0.0)
    over_e = jnp.where(inside, 1.0 / (permit + loss), 0.0)
    return (
        (1.0 - loss) * over_h,
        time_step * over_h,
        (permit - loss) * over_e,
        time_step * over_e,
        jnp.where(metal, 1.0, 0.0),
    )


def magnetic_new(h, e, ey, ez, ex, keep, push):
    curl = (
        (ey[2] - e[2]) - (ez[1] - e[1]),
        (ez[0] - e[0]) - (ex[2] - e[2]),
        (ex[1] - e[1]) - (ey[0] - e[0]),
    )
    return [None if h[k] is None else keep * h[k] - push * curl[k] for k in range(3)]


def electric_new(e, h, hy, hz, hx, drag, keep, push):
    curl = (
        (h[2] - hy[2]) - (h[1] - hz[1]),
        (h[0] - hz[0]) - (h[2] - hx[2]),
        (h[1] - hx[1]) - (h[0] - hy[0]),
    )
    return [keep * e[k] + push * (curl[k] - drag[k]) for k in range(3)]


def both_steps(flags, wide, before, after, own, left, right, polar, e_out, h_out, p_out, j_out, h1, e1, h2):
    plane = planes_of(flags, wide, before, after)
    lane = lanes()
    side = (lane % 4) < 2

    edge = []
    for g in range(3):
        low = jnp.where(side, left[g], own[g])
        high = jnp.where(side, own[g], right[g])
        for k in range(4):
            edge.append(jnp.where(lane < SPAN, roll(low, -SPAN * k, 1), roll(high, SPAN - SPAN * k, 1)))
    x_next = lambda a: roll(a, -1, 1)
    x_back = lambda a: roll(a, 1, 1)
    y_next = lambda a: roll(a, -1, 0)
    y_back = lambda a: roll(a, 1, 0)
    z_next = lambda a: roll(a, -4, 1)
    z_back = lambda a: roll(a, 4, 1)

    def nexts(f):
        return (
            {0: y_next(f[0]), 2: y_next(f[2])},
            {0: z_next(f[0]), 1: z_next(f[1])},
            {1: x_next(f[1]), 2: x_next(f[2])},
        )

    def backs(f):
        return (
            {0: y_back(f[0]), 2: y_back(f[2])},
            {0: z_back(f[0]), 1: z_back(f[1])},
            {1: x_back(f[1]), 2: x_back(f[2])},
        )

    keep_h, push_h, keep_e, push_e, metal = factors(edge[CODE])
    ce0 = edge[EX : EZ + 1]
    ch1 = magnetic_new(edge[HX : HZ + 1], ce0, *nexts(ce0), keep_h, push_h)
    drag = [metal * (edge[QX + k] + GAIN * ce0[k]) for k in range(3)]
    ce1 = electric_new(ce0, ch1, *backs(ch1), drag, keep_e, push_e)
    ch2 = magnetic_new(ch1, ce1, *nexts(ce1), keep_h, push_h)

    def after_x(array, z, column):
        return jnp.where(lane == 127, roll(column, 127 - (SPAN + 4 * (z + 2) + 2), 1), roll(array, -1, 1))

    def before_x(array, z, column):
        return jnp.where(lane == 0, roll(column, -(4 * (z + 2) + 1), 1), roll(array, 1, 1))

    for z in range(-2, 5):
        e = [plane(EX + k, z) for k in range(3)]
        up = [plane(EX + k, z + 1) for k in range(2)]
        h = [plane(HX + k, z) for k in range(3)]
        keep_h, push_h, _, _, _ = factors(plane(CODE, z))
        new = magnetic_new(
            h,
            e,
            {0: y_next(e[0]), 2: y_next(e[2])},
            {0: up[0], 1: up[1]},
            {1: after_x(e[1], z, ce0[1]), 2: after_x(e[2], z, ce0[2])},
            keep_h,
            push_h,
        )
        for k in range(3):
            if new[k] is not None:
                h1[z + 2, k] = new[k]
    for z in range(-1, 5):
        e = [plane(EX + k, z) for k in range(3)]
        h = [h1[z + 2, k] for k in range(3)]
        down = [h1[z + 1, k] for k in range(2)]
        _, _, keep_e, push_e, metal = factors(plane(CODE, z))
        held = [plane(QX + k, z) for k in range(3)]
        flow = [None if held[k] is None else held[k] + GAIN * metal * e[k] for k in range(3)]
        if 0 <= z < 4:
            for k in range(3):
                j_out[k, z] = flow[k][0:16]
        new = electric_new(
            e,
            h,
            {0: y_back(h[0]), 2: y_back(h[2])},
            {0: down[0], 1: down[1]},
            {1: before_x(h[1], z, ch1[1]), 2: before_x(h[2], z, ch1[2])},
            [0.0 if flow[k] is None else metal * flow[k] for k in range(3)],
            keep_e,
            push_e,
        )
        for k in range(3):
            e1[z + 1, k] = new[k]
    for z in range(-1, 4):
        e = [e1[z + 1, k] for k in range(3)]
        up = [e1[z + 2, k] for k in range(2)]
        h = [h1[z + 2, k] for k in range(3)]
        keep_h, push_h, _, _, _ = factors(plane(CODE, z))
        new = magnetic_new(
            h,
            e,
            {0: y_next(e[0]), 2: y_next(e[2])},
            {0: up[0], 1: up[1]},
            {1: after_x(e[1], z, ce1[1]), 2: after_x(e[2], z, ce1[2])},
            keep_h,
            push_h,
        )
        for k in range(3):
            h2[z + 1, k] = new[k]
            if z >= 0:
                h_out[k, z] = new[k][0:16]
    for z in range(4):
        h = [h2[z + 1, k] for k in range(3)]
        down = [h2[z, k] for k in range(2)]
        _, _, keep_e, push_e, metal = [f[0:16] for f in factors(plane(CODE, z))]
        e = [e1[z + 1, k][0:16] for k in range(3)]
        drag = []
        for k in range(3):
            flow = j_out[k, z]
            bound = polar[k, z] + time_step * flow
            flow = HOLD * flow - PULL * bound + GAIN * metal * e[k]
            j_out[k, z] = flow
            p_out[k, z] = bound + time_step * flow
            drag.append(metal * flow)
        new = electric_new(
            e,
            [a[0:16] for a in h],
            {0: y_back(h[0])[0:16], 2: y_back(h[2])[0:16]},
            {0: down[0][0:16], 1: down[1][0:16]},
            {1: before_x(h[1], z, ch2[1])[0:16], 2: before_x(h[2], z, ch2[2])[0:16]},
            drag,
            keep_e,
            push_e,
        )
        for k in range(3):
            e_out[k, z] = new[k]


VMEM = pl.BlockSpec(memory_space=pltpu.VMEM)
SMEM = pl.BlockSpec(memory_space=pltpu.SMEM)


def call(kernel, outs, args, scratch=(), flops=0, name=None):
    size = sum(a.size for a in args) + sum(o.size for o in outs)
    return pl.pallas_call(
        kernel,
        out_shape=outs,
        in_specs=[SMEM if a.ndim == 1 else VMEM for a in args],
        out_specs=[VMEM] * len(outs),
        scratch_shapes=list(scratch),
        cost_estimate=pl.CostEstimate(flops=flops, bytes_accessed=4 * size, transcendentals=0),
        compiler_params=pltpu.CompilerParams(vmem_limit_bytes=16 * 2**20),
        name=name,
    )(*args)


def f32(*shape):
    return jax.ShapeDtypeStruct(shape, jnp.float32)


def on_device(electric, magnetic, polar, current, material, pml):
    cells = (electric, magnetic, polar, current, material, pml)
    gx, gy, gz = (lax.axis_size(a) for a in ("gx", "gy", "gz"))
    place = lax.axis_index("gz")
    flags = jnp.stack([place, gz - 1 - place]).astype(jnp.int32)

    up, down = call(y_faces, [f32(64, 128), f32(48, 128)], cells, name="y_faces")
    before = lax.ppermute(up, "gy", up_of(gy))
    after = lax.ppermute(down, "gy", down_of(gy))

    wide, up, down = call(
        z_faces,
        [f32(4, 10, ROWS, 128), f32(16, ROWS, 128), f32(11, ROWS, 128)],
        (*cells, before, after),
        name="z_faces",
    )
    before = lax.ppermute(up, "gz", [(i, (i + 1) % gz) for i in range(gz)])
    after = lax.ppermute(down, "gz", [((i + 1) % gz, i) for i in range(gz)])

    (own,) = call(x_edges, [f32(3, ROWS, 128)], (flags, wide, before, after), name="x_edges")
    left = lax.ppermute(own, "gx", up_of(gx))
    right = lax.ppermute(own, "gx", down_of(gx))

    return tuple(
        call(
            both_steps,
            [f32(3, 4, 16, 128)] * 4,
            (flags, wide, before, after, own, left, right, polar),
            scratch=[
                pltpu.VMEM((7, 3, ROWS, 128), jnp.float32),
                pltpu.VMEM((6, 3, ROWS, 128), jnp.float32),
                pltpu.VMEM((5, 3, ROWS, 128), jnp.float32),
            ],
            flops=4_000_000,
            name="both_steps",
        )
    )


def solution(mesh):
    fields = P(None, "gz", "gy", "gx")
    cells = P("gz", "gy", "gx")
    return jax.shard_map(
        on_device,
        mesh=mesh,
        in_specs=(fields, fields, fields, fields, cells, cells),
        out_specs=(fields, fields, fields, fields),
        check_vma=False,
    )
```

```python
import jax
import jax.numpy as jnp
from jax import lax
from jax.experimental import pallas as pl
from jax.experimental.pallas import tpu as pltpu
from jax.sharding import PartitionSpec as P

time_step = 0.5
damping = 0.2
omega_sq = 1.0
strength = 3.0

DECAY = 1.0 + 0.5 * damping * time_step
HOLD = (1.0 - 0.5 * damping * time_step) / DECAY
PULL = time_step * omega_sq / DECAY
GAIN = PULL * strength

EX, EY, EZ, HX, HY, HZ, QX, QY, QZ, CODE = range(10)
EVERY = tuple(range(10))

Y_UP = [(c, 14) for c in (EX, EY, EZ, HX, HZ, CODE)] + [(c, 15) for c in EVERY]
Y_DOWN = [(c, 0) for c in (EX, EY, EZ, HX, HY, HZ, QX, QZ, CODE)] + [(EX, 1), (EZ, 1)]
Z_UP = [(c, 2) for c in (EX, EY, EZ, HX, HY, CODE)] + [(c, 3) for c in EVERY]
Z_DOWN = [(c, 0) for c in (EX, EY, EZ, HX, HY, HZ, QX, QY, CODE)] + [(EX, 1), (EY, 1)]

ROWS = 24
PLANES = range(-2, 6)
SPAN = 32
HINT = 1 << 26


def up_of(n):
    return [(i, i + 1) for i in range(n - 1)]


def down_of(n):
    return [(i + 1, i) for i in range(n - 1)]


def code_of(material, pml):
    return (1 + 4 * material + pml).astype(jnp.float32)


def y_face(cells, c, row):
    e, h, p, j, material, pml = cells
    if c < HX:
        return e[c, :, row, :]
    if c < QX:
        return h[c - HX, :, row, :]
    if c < CODE:
        return HOLD * j[c - QX, :, row, :] - PULL * p[c - QX, :, row, :]
    return code_of(material[:, row, :], pml[:, row, :])


def load_and_low_faces(*refs):
    far, near, down, done = refs[:6], refs[6:12], refs[12], refs[13]
    copies = [pltpu.make_async_copy(a, b, done.at[i]) for i, (a, b) in enumerate(zip(far, near))]
    for copy in copies:
        copy.start()
    for copy in copies:
        copy.wait()
    down[...] = jnp.zeros_like(down)
    for i, (c, row) in enumerate(Y_DOWN):
        down[4 * i : 4 * i + 4, :] = y_face(near, c, row)


def high_faces(*refs):
    near, _, up = refs[:6], refs[6], refs[7]
    for i, (c, row) in enumerate(Y_UP):
        up[4 * i : 4 * i + 4, :] = y_face(near, c, row)


def again(down, _, copy):
    copy[...] = down[0:48, :]


def z_faces(e, h, p, j, material, pml, before, after, later, wide, up, down):
    for z in range(4):
        for c in EVERY:
            if c < HX:
                own = e[c, z]
            elif c < QX:
                own = h[c - HX, z]
            elif c < CODE:
                own = HOLD * j[c - QX, z] - PULL * p[c - QX, z]
            else:
                own = code_of(material[z], pml[z])
            wide[z, c, 0:16, :] = own
            wide[z, c, 16:24, :] = jnp.zeros((8, 128), jnp.float32)
        for i, (c, row) in enumerate(Y_UP):
            wide[z, c, row + 8 : row + 9, :] = before[4 * i + z : 4 * i + z + 1, :]
        for i, (c, row) in enumerate(Y_DOWN):
            at = slice(4 * i + z, 4 * i + z + 1)
            wide[z, c, row + 16 : row + 17, :] = after[at, :] + later[at, :]
    for i, (c, z) in enumerate(Z_UP):
        up[i] = wide[z, c]
    for i, (c, z) in enumerate(Z_DOWN):
        down[i] = wide[z, c]


def planes_of(flags, wide, before, after):
    first = flags[0] == 0
    last = flags[1] == 0

    def plane(c, z):
        if 0 <= z < 4:
            return wide[z, c]
        if z < 0:
            if (c, z + 4) not in Z_UP:
                return None
            got = before[Z_UP.index((c, z + 4))]
            return jnp.where(first, 0.0, got)
        if (c, z - 4) not in Z_DOWN:
            return None
        got = after[Z_DOWN.index((c, z - 4))]
        return jnp.where(last, 0.0, got)

    return plane


def lanes():
    return lax.broadcasted_iota(jnp.int32, (ROWS, 128), 1)


def roll(array, shift, axis):
    shift = shift % array.shape[axis]
    return pltpu.roll(array, shift, axis) if shift else array


def x_edges(flags, wide, before, after, edges):
    plane = planes_of(flags, wide, before, after)
    lane = lanes()
    for g in range(3):
        total = jnp.zeros((ROWS, 128), jnp.float32)
        for c in range(4 * g, min(4 * g + 4, 10)):
            for z in PLANES:
                value = plane(c, z)
                if value is None:
                    continue
                at = SPAN * (c - 4 * g) + 4 * (z + 2)
                moved = roll(value, at - 126, 1)
                total = jnp.where((lane >= at) & (lane < at + 4), moved, total)
        edges[g] = total


def factors(code):
    metal = code > 8.5
    dielec = (code > 4.5) & (code < 8.5)
    inside = code > 0.5
    level = code - jnp.where(metal, 9.0, jnp.where(dielec, 5.0, 1.0))
    loss = jnp.where(level > 2.5, 0.25, jnp.where(level > 1.5, 0.1, jnp.where(level > 0.5, 0.025, 0.0)))
    permit = jnp.where(metal, 1.5, jnp.where(dielec, 2.25, 1.0))
    over_h = jnp.where(inside, 1.0 / (1.0 + loss), 0.0)
    over_e = jnp.where(inside, 1.0 / (permit + loss), 0.0)
    return (
        (1.0 - loss) * over_h,
        time_step * over_h,
        (permit - loss) * over_e,
        time_step * over_e,
        jnp.where(metal, 1.0, 0.0),
    )


def magnetic_new(h, e, ey, ez, ex, keep, push):
    curl = (
        (ey[2] - e[2]) - (ez[1] - e[1]),
        (ez[0] - e[0]) - (ex[2] - e[2]),
        (ex[1] - e[1]) - (ey[0] - e[0]),
    )
    return [None if h[k] is None else keep * h[k] - push * curl[k] for k in range(3)]


def electric_new(e, h, hy, hz, hx, drag, keep, push):
    curl = (
        (h[2] - hy[2]) - (h[1] - hz[1]),
        (h[0] - hz[0]) - (h[2] - hx[2]),
        (h[1] - hx[1]) - (h[0] - hy[0]),
    )
    return [keep * e[k] + push * (curl[k] - drag[k]) for k in range(3)]


def both_steps(flags, wide, before, after, own, left, right, polar, e_out, h_out, p_out, j_out, h1, e1, h2):
    plane = planes_of(flags, wide, before, after)
    lane = lanes()
    side = (lane % 4) < 2

    edge = []
    for g in range(3):
        low = jnp.where(side, left[g], own[g])
        high = jnp.where(side, own[g], right[g])
        for k in range(4):
            edge.append(jnp.where(lane < SPAN, roll(low, -SPAN * k, 1), roll(high, SPAN - SPAN * k, 1)))
    x_next = lambda a: roll(a, -1, 1)
    x_back = lambda a: roll(a, 1, 1)
    y_next = lambda a: roll(a, -1, 0)
    y_back = lambda a: roll(a, 1, 0)
    z_next = lambda a: roll(a, -4, 1)
    z_back = lambda a: roll(a, 4, 1)

    def nexts(f):
        return (
            {0: y_next(f[0]), 2: y_next(f[2])},
            {0: z_next(f[0]), 1: z_next(f[1])},
            {1: x_next(f[1]), 2: x_next(f[2])},
        )

    def backs(f):
        return (
            {0: y_back(f[0]), 2: y_back(f[2])},
            {0: z_back(f[0]), 1: z_back(f[1])},
            {1: x_back(f[1]), 2: x_back(f[2])},
        )

    keep_h, push_h, keep_e, push_e, metal = factors(edge[CODE])
    ce0 = edge[EX : EZ + 1]
    ch1 = magnetic_new(edge[HX : HZ + 1], ce0, *nexts(ce0), keep_h, push_h)
    drag = [metal * (edge[QX + k] + GAIN * ce0[k]) for k in range(3)]
    ce1 = electric_new(ce0, ch1, *backs(ch1), drag, keep_e, push_e)
    ch2 = magnetic_new(ch1, ce1, *nexts(ce1), keep_h, push_h)

    def after_x(array, z, column):
        return jnp.where(lane == 127, roll(column, 127 - (SPAN + 4 * (z + 2) + 2), 1), roll(array, -1, 1))

    def before_x(array, z, column):
        return jnp.where(lane == 0, roll(column, -(4 * (z + 2) + 1), 1), roll(array, 1, 1))

    for z in range(-2, 5):
        e = [plane(EX + k, z) for k in range(3)]
        up = [plane(EX + k, z + 1) for k in range(2)]
        h = [plane(HX + k, z) for k in range(3)]
        keep_h, push_h, _, _, _ = factors(plane(CODE, z))
        new = magnetic_new(
            h,
            e,
            {0: y_next(e[0]), 2: y_next(e[2])},
            {0: up[0], 1: up[1]},
            {1: after_x(e[1], z, ce0[1]), 2: after_x(e[2], z, ce0[2])},
            keep_h,
            push_h,
        )
        for k in range(3):
            if new[k] is not None:
                h1[z + 2, k] = new[k]
    for z in range(-1, 5):
        e = [plane(EX + k, z) for k in range(3)]
        h = [h1[z + 2, k] for k in range(3)]
        down = [h1[z + 1, k] for k in range(2)]
        _, _, keep_e, push_e, metal = factors(plane(CODE, z))
        held = [plane(QX + k, z) for k in range(3)]
        flow = [None if held[k] is None else held[k] + GAIN * metal * e[k] for k in range(3)]
        if 0 <= z < 4:
            for k in range(3):
                j_out[k, z] = flow[k][0:16]
        new = electric_new(
            e,
            h,
            {0: y_back(h[0]), 2: y_back(h[2])},
            {0: down[0], 1: down[1]},
            {1: before_x(h[1], z, ch1[1]), 2: before_x(h[2], z, ch1[2])},
            [0.0 if flow[k] is None else metal * flow[k] for k in range(3)],
            keep_e,
            push_e,
        )
        for k in range(3):
            e1[z + 1, k] = new[k]
    for z in range(-1, 4):
        e = [e1[z + 1, k] for k in range(3)]
        up = [e1[z + 2, k] for k in range(2)]
        h = [h1[z + 2, k] for k in range(3)]
        keep_h, push_h, _, _, _ = factors(plane(CODE, z))
        new = magnetic_new(
            h,
            e,
            {0: y_next(e[0]), 2: y_next(e[2])},
            {0: up[0], 1: up[1]},
            {1: after_x(e[1], z, ce1[1]), 2: after_x(e[2], z, ce1[2])},
            keep_h,
            push_h,
        )
        for k in range(3):
            h2[z + 1, k] = new[k]
            if z >= 0:
                h_out[k, z] = new[k][0:16]
    for z in range(4):
        h = [h2[z + 1, k] for k in range(3)]
        down = [h2[z, k] for k in range(2)]
        _, _, keep_e, push_e, metal = [f[0:16] for f in factors(plane(CODE, z))]
        e = [e1[z + 1, k][0:16] for k in range(3)]
        drag = []
        for k in range(3):
            flow = j_out[k, z]
            bound = polar[k, z] + time_step * flow
            flow = HOLD * flow - PULL * bound + GAIN * metal * e[k]
            j_out[k, z] = flow
            p_out[k, z] = bound + time_step * flow
            drag.append(metal * flow)
        new = electric_new(
            e,
            [a[0:16] for a in h],
            {0: y_back(h[0])[0:16], 2: y_back(h[2])[0:16]},
            {0: down[0][0:16], 1: down[1][0:16]},
            {1: before_x(h[1], z, ch2[1])[0:16], 2: before_x(h[2], z, ch2[2])[0:16]},
            drag,
            keep_e,
            push_e,
        )
        for k in range(3):
            e_out[k, z] = new[k]


VMEM = pl.BlockSpec(memory_space=pltpu.VMEM)
SMEM = pl.BlockSpec(memory_space=pltpu.SMEM)
HBM = pl.BlockSpec(memory_space=pltpu.HBM)


def call(kernel, outs, args, scratch=(), flops=0, size=0, far=False, name=None):
    size = size or sum(a.size for a in args) + sum(o.size for o in outs)
    return pl.pallas_call(
        kernel,
        out_shape=outs,
        in_specs=[HBM if far else SMEM if a.ndim == 1 else VMEM for a in args],
        out_specs=[VMEM] * len(outs),
        scratch_shapes=list(scratch),
        cost_estimate=pl.CostEstimate(flops=flops, bytes_accessed=4 * size, transcendentals=0),
        compiler_params=pltpu.CompilerParams(vmem_limit_bytes=16 * 2**20),
        name=name,
    )(*args)


def f32(*shape):
    return jax.ShapeDtypeStruct(shape, jnp.float32)


def on_device(electric, magnetic, polar, current, material, pml):
    cells = (electric, magnetic, polar, current, material, pml)
    gx, gy, gz = (lax.axis_size(a) for a in ("gx", "gy", "gz"))
    place = lax.axis_index("gz")
    flags = jnp.stack([place, gz - 1 - place]).astype(jnp.int32)

    shapes = [jax.ShapeDtypeStruct(a.shape, a.dtype) for a in cells]
    cells = [pltpu.with_memory_space_constraint(a, pltpu.HBM) for a in cells]
    *cells, down = call(
        load_and_low_faces,
        [*shapes, f32(72, 128)],
        cells,
        scratch=[pltpu.SemaphoreType.DMA((6,))],
        far=True,
        name="load_and_low_faces",
    )
    near = [(i, j) for i, j in down_of(gy) if i % 4 in (1, 2)]
    rest = [(i, j) for i, j in down_of(gy) if i % 4 in (0, 3)]
    after = lax.ppermute(down, "gy", near)
    (up,) = call(high_faces, [f32(64, 128)], (*cells, down), size=HINT, name="high_faces")
    before = lax.ppermute(up, "gy", up_of(gy))
    (down,) = call(again, [f32(48, 128)], (down, up), size=HINT, name="again")
    later = lax.ppermute(down, "gy", rest)

    wide, up, down = call(
        z_faces,
        [f32(4, 10, ROWS, 128), f32(16, ROWS, 128), f32(11, ROWS, 128)],
        (*cells, before, after, later),
        name="z_faces",
    )
    before = lax.ppermute(up, "gz", [(i, (i + 1) % gz) for i in range(gz)])
    after = lax.ppermute(down, "gz", [((i + 1) % gz, i) for i in range(gz)])

    (own,) = call(x_edges, [f32(3, ROWS, 128)], (flags, wide, before, after), name="x_edges")
    left = lax.ppermute(own, "gx", up_of(gx))
    right = lax.ppermute(own, "gx", down_of(gx))

    return tuple(
        call(
            both_steps,
            [f32(3, 4, 16, 128)] * 4,
            (flags, wide, before, after, own, left, right, polar),
            scratch=[
                pltpu.VMEM((7, 3, ROWS, 128), jnp.float32),
                pltpu.VMEM((6, 3, ROWS, 128), jnp.float32),
                pltpu.VMEM((5, 3, ROWS, 128), jnp.float32),
            ],
            flops=4_000_000,
            name="both_steps",
        )
    )


def solution(mesh):
    fields = P(None, "gz", "gy", "gx")
    cells = P("gz", "gy", "gx")
    return jax.shard_map(
        on_device,
        mesh=mesh,
        in_specs=(fields, fields, fields, fields, cells, cells),
        out_specs=(fields, fields, fields, fields),
        check_vma=False,
    )
```

```python
import jax
import jax.numpy as jnp
from jax import lax
from jax.experimental import pallas as pl
from jax.experimental.pallas import tpu as pltpu
from jax.sharding import PartitionSpec as P

time_step = 0.5
damping = 0.2
omega_sq = 1.0
strength = 3.0

DECAY = 1.0 + 0.5 * damping * time_step
HOLD = (1.0 - 0.5 * damping * time_step) / DECAY
PULL = time_step * omega_sq / DECAY
GAIN = PULL * strength

EX, EY, EZ, HX, HY, HZ, QX, QY, QZ, CODE = range(10)
EVERY = tuple(range(10))

Y_UP = [(c, 14) for c in (EX, EY, EZ, HX, HZ, CODE)] + [(c, 15) for c in EVERY]
Y_DOWN = [(c, 0) for c in (EX, EY, EZ, HX, HY, HZ, QX, QZ, CODE)] + [(EX, 1), (EZ, 1)]
Z_UP = [(c, 2) for c in (EX, EY, EZ, HX, HY, CODE)] + [(c, 3) for c in EVERY]
Z_DOWN = [(c, 0) for c in (EX, EY, EZ, HX, HY, HZ, QX, QY, CODE)] + [(EX, 1), (EY, 1)]

ROWS = 24
PLANES = range(-2, 6)
SPAN = 32
HINT = 1 << 26


def up_of(n):
    return [(i, i + 1) for i in range(n - 1)]


def down_of(n):
    return [(i + 1, i) for i in range(n - 1)]


def code_of(material, pml):
    return (1 + 4 * material + pml).astype(jnp.float32)


def y_face(cells, c, row):
    e, h, p, j, material, pml = cells
    if c < HX:
        return e[c, :, row, :]
    if c < QX:
        return h[c - HX, :, row, :]
    if c < CODE:
        return HOLD * j[c - QX, :, row, :] - PULL * p[c - QX, :, row, :]
    return code_of(material[:, row, :], pml[:, row, :])


def load_and_low_faces(*refs):
    far, near, down, done = refs[:6], refs[6:12], refs[12], refs[13]
    copies = [pltpu.make_async_copy(a, b, done.at[i]) for i, (a, b) in enumerate(zip(far, near))]
    for copy in copies:
        copy.start()
    for copy in copies:
        copy.wait()
    down[...] = jnp.zeros_like(down)
    for i, (c, row) in enumerate(Y_DOWN):
        down[4 * i : 4 * i + 4, :] = y_face(near, c, row)


def high_faces(*refs):
    near, _, up = refs[:6], refs[6], refs[7]
    for i, (c, row) in enumerate(Y_UP):
        up[4 * i : 4 * i + 4, :] = y_face(near, c, row)


def again(down, _, copy):
    copy[...] = down[0:48, :]


def widen_rows(e, h, p, j, material, pml, before, after, later, wide, edges):
    lane = lanes()
    for z in range(4):
        for c in EVERY:
            if c < HX:
                own = e[c, z]
            elif c < QX:
                own = h[c - HX, z]
            elif c < CODE:
                own = HOLD * j[c - QX, z] - PULL * p[c - QX, z]
            else:
                own = code_of(material[z], pml[z])
            wide[z, c, 0:16, :] = own
            wide[z, c, 16:24, :] = jnp.zeros((8, 128), jnp.float32)
        for i, (c, row) in enumerate(Y_UP):
            wide[z, c, row + 8 : row + 9, :] = before[4 * i + z : 4 * i + z + 1, :]
        for i, (c, row) in enumerate(Y_DOWN):
            at = slice(4 * i + z, 4 * i + z + 1)
            wide[z, c, row + 16 : row + 17, :] = after[at, :] + later[at, :]
    for g in range(3):
        total = jnp.zeros((ROWS, 128), jnp.float32)
        for c in range(4 * g, min(4 * g + 4, 10)):
            for z in range(4):
                at = SPAN * (c - 4 * g) + 4 * (z + 2)
                moved = roll(wide[z, c], at - 126, 1)
                total = jnp.where((lane >= at) & (lane < at + 4), moved, total)
        edges[g] = total


def z_faces(wide, _, up, down):
    for i, (c, z) in enumerate(Z_UP):
        up[i] = wide[z, c]
    for i, (c, z) in enumerate(Z_DOWN):
        down[i] = wide[z, c]


def sides(own, left, right, g):
    near = (lanes() % 4) < 2
    return jnp.where(near, left[g], own[g]), jnp.where(near, own[g], right[g])


def columns_on(own, left, right, out):
    part = (lanes() % SPAN) // 8
    for g in range(3):
        low, high = sides(own, left, right, g)
        up = jnp.where(part == 0, roll(low, -16, 1), roll(high, -8, 1))
        down = jnp.where(part == 2, roll(high, 8, 1), roll(low, 16, 1))
        out[g] = jnp.where(part < 2, up, down)


def grid_ends():
    place = lax.axis_index("gz")
    return place == 0, place == lax.axis_size("gz") - 1


def planes_of(wide, before, after):
    first, last = grid_ends()

    def plane(c, z):
        if 0 <= z < 4:
            return wide[z, c]
        if z < 0:
            if (c, z + 4) not in Z_UP:
                return None
            got = before[Z_UP.index((c, z + 4))]
            return jnp.where(first, 0.0, got)
        if (c, z - 4) not in Z_DOWN:
            return None
        got = after[Z_DOWN.index((c, z - 4))]
        return jnp.where(last, 0.0, got)

    return plane


def lanes():
    return lax.broadcasted_iota(jnp.int32, (ROWS, 128), 1)


def roll(array, shift, axis):
    shift = shift % array.shape[axis]
    return pltpu.roll(array, shift, axis) if shift else array


def factors(code):
    metal = code > 8.5
    dielec = (code > 4.5) & (code < 8.5)
    inside = code > 0.5
    level = code - jnp.where(metal, 9.0, jnp.where(dielec, 5.0, 1.0))
    loss = jnp.where(level > 2.5, 0.25, jnp.where(level > 1.5, 0.1, jnp.where(level > 0.5, 0.025, 0.0)))
    permit = jnp.where(metal, 1.5, jnp.where(dielec, 2.25, 1.0))
    over_h = jnp.where(inside, 1.0 / (1.0 + loss), 0.0)
    over_e = jnp.where(inside, 1.0 / (permit + loss), 0.0)
    return (
        (1.0 - loss) * over_h,
        time_step * over_h,
        (permit - loss) * over_e,
        time_step * over_e,
        jnp.where(metal, 1.0, 0.0),
    )


def magnetic_new(h, e, ey, ez, ex, keep, push):
    curl = (
        (ey[2] - e[2]) - (ez[1] - e[1]),
        (ez[0] - e[0]) - (ex[2] - e[2]),
        (ex[1] - e[1]) - (ey[0] - e[0]),
    )
    return [None if h[k] is None else keep * h[k] - push * curl[k] for k in range(3)]


def electric_new(e, h, hy, hz, hx, drag, keep, push):
    curl = (
        (h[2] - hy[2]) - (h[1] - hz[1]),
        (h[0] - hz[0]) - (h[2] - hx[2]),
        (h[1] - hx[1]) - (h[0] - hy[0]),
    )
    return [keep * e[k] + push * (curl[k] - drag[k]) for k in range(3)]


x_next = lambda a: roll(a, -1, 1)
x_back = lambda a: roll(a, 1, 1)
y_next = lambda a: roll(a, -1, 0)
y_back = lambda a: roll(a, 1, 0)


def first_step(wide, before, after, polar, h1, e1, p1, j1, fh, fe):
    plane = planes_of(wide, before, after)
    for z in range(-2, 5):
        e = [plane(EX + k, z) for k in range(3)]
        up = [plane(EX + k, z + 1) for k in range(2)]
        h = [plane(HX + k, z) for k in range(3)]
        keep_h, push_h, keep_e, push_e, metal = factors(plane(CODE, z))
        new = magnetic_new(
            h,
            e,
            {0: y_next(e[0]), 2: y_next(e[2])},
            {0: up[0], 1: up[1]},
            {1: x_next(e[1]), 2: x_next(e[2])},
            keep_h,
            push_h,
        )
        for k in range(3):
            if new[k] is not None:
                h1[z + 2, k] = new[k]
        if -1 <= z < 4:
            fh[z + 1, 0] = keep_h
            fh[z + 1, 1] = push_h
        if 0 <= z < 4:
            for k, f in enumerate((keep_e, push_e, metal)):
                fe[z, k] = f[0:16]
        if z == -2:
            continue
        h = new
        down = [h1[z + 1, k] for k in range(2)]
        held = [plane(QX + k, z) for k in range(3)]
        flow = [None if held[k] is None else held[k] + GAIN * metal * e[k] for k in range(3)]
        if 0 <= z < 4:
            for k in range(3):
                j1[k, z] = flow[k][0:16]
                p1[k, z] = polar[k, z] + time_step * flow[k][0:16]
        new = electric_new(
            e,
            h,
            {0: y_back(h[0]), 2: y_back(h[2])},
            {0: down[0], 1: down[1]},
            {1: x_back(h[1]), 2: x_back(h[2])},
            [0.0 if flow[k] is None else metal * flow[k] for k in range(3)],
            keep_e,
            push_e,
        )
        for k in range(3):
            e1[z + 1, k] = new[k]


def columns(own, left, right, before, after):
    first, last = grid_ends()
    lane = lanes()
    part = (lane % SPAN) // 8
    values = []
    for g in range(3):
        low, high = sides(own, left, right, g)
        up = jnp.where(first, 0.0, before[g])
        down = jnp.where(last, 0.0, after[g])
        low = jnp.where(part == 0, up, jnp.where(part == 3, down, low))
        high = jnp.where(part == 0, roll(up, -8, 1), jnp.where(part == 3, roll(down, 8, 1), high))
        for k in range(4):
            values.append(jnp.where(lane < SPAN, roll(low, -SPAN * k, 1), roll(high, SPAN - SPAN * k, 1)))
    z_next = lambda a: roll(a, -4, 1)
    z_back = lambda a: roll(a, 4, 1)

    def shifted(f, y, z, x):
        return {0: y(f[0]), 2: y(f[2])}, {0: z(f[0]), 1: z(f[1])}, {1: x(f[1]), 2: x(f[2])}

    keep_h, push_h, keep_e, push_e, metal = factors(values[CODE])
    e0 = values[EX : EZ + 1]
    h1 = magnetic_new(values[HX : HZ + 1], e0, *shifted(e0, y_next, z_next, x_next), keep_h, push_h)
    drag = [metal * (values[QX + k] + GAIN * e0[k]) for k in range(3)]
    e1 = electric_new(e0, h1, *shifted(h1, y_back, z_back, x_back), drag, keep_e, push_e)
    h2 = magnetic_new(h1, e1, *shifted(e1, y_next, z_next, x_next), keep_h, push_h)
    return h1, e1, h2


def second_step(own, left, right, before, after, h1, e1, p1, j1, fh, fe, *rest):
    outs, near, h2, done = rest[:4], rest[4:8], rest[8], rest[9]
    e_near, h_near, p_near, j_near = near
    lane = lanes()
    ch1, ce1, ch2 = columns(own, left, right, before, after)

    def at_ends(column):
        return jnp.where(lane % 4 == 1, roll(column, -SPAN, 1), column)

    def put_right(array, z, column):
        return jnp.where((lane == 0) | (lane == 127), roll(column, 127 - (4 * (z + 2) + 1), 1), array)

    ends_h = [at_ends(a) for a in ch1]
    ends_e = [at_ends(a) for a in ce1]

    def after_x(array, z):
        return lambda k: jnp.where(lane == 127, roll(ce1[k], 127 - (SPAN + 4 * (z + 2) + 2), 1), x_next(array[k]))

    def before_x(array, z):
        return lambda k: jnp.where(lane == 0, roll(ch2[k], -(4 * (z + 2) + 1), 1), x_back(array[k]))

    def fixed_e(z):
        return [put_right(e1[z + 1, k], z, ends_e[k]) for k in range(3)]

    copies = [pltpu.make_async_copy(a, b, done.at[i]) for i, (a, b) in enumerate(zip(near, outs))]
    for z in range(4):
        metal = fe[z, 2]
        for k in range(3):
            e = put_right(e1[z + 1, k], z, ends_e[k])[0:16]
            flow = HOLD * j1[k, z] - PULL * p1[k, z] + GAIN * metal * e
            j_near[k, z] = flow
            p_near[k, z] = p1[k, z] + time_step * flow
    copies[2].start()
    copies[3].start()
    e = fixed_e(-1)
    for z in range(-1, 4):
        up = fixed_e(z + 1)
        h = [h1[z + 2, 0]] + [put_right(h1[z + 2, k], z, ends_h[k]) for k in (1, 2)]
        x = after_x(e, z)
        new = magnetic_new(
            h,
            e,
            {0: y_next(e[0]), 2: y_next(e[2])},
            {0: up[0], 1: up[1]},
            {1: x(1), 2: x(2)},
            fh[z + 1, 0],
            fh[z + 1, 1],
        )
        for k in range(3):
            h2[z + 1, k] = new[k]
            if z >= 0:
                h_near[k, z] = new[k][0:16]
        e = up
    copies[1].start()
    for z in range(4):
        h = [h2[z + 1, k] for k in range(3)]
        down = [h2[z, k] for k in range(2)]
        x = before_x(h, z)
        new = electric_new(
            [a[0:16] for a in fixed_e(z)],
            [a[0:16] for a in h],
            {0: y_back(h[0])[0:16], 2: y_back(h[2])[0:16]},
            {0: down[0][0:16], 1: down[1][0:16]},
            {1: x(1)[0:16], 2: x(2)[0:16]},
            [fe[z, 2] * j_near[k, z] for k in range(3)],
            fe[z, 0],
            fe[z, 1],
        )
        for k in range(3):
            e_near[k, z] = new[k]
    copies[0].start()
    for copy in copies:
        copy.wait()


VMEM = pl.BlockSpec(memory_space=pltpu.VMEM)
HBM = pl.BlockSpec(memory_space=pltpu.HBM)


def call(kernel, outs, args, scratch=(), flops=0, size=0, far=False, far_out=False, name=None):
    size = size or sum(a.size for a in args) + sum(o.size for o in outs)
    return pl.pallas_call(
        kernel,
        out_shape=outs,
        in_specs=[HBM if far else VMEM] * len(args),
        out_specs=[HBM if far_out else VMEM] * len(outs),
        scratch_shapes=list(scratch),
        cost_estimate=pl.CostEstimate(flops=flops, bytes_accessed=4 * size, transcendentals=0),
        compiler_params=pltpu.CompilerParams(vmem_limit_bytes=16 * 2**20),
        name=name,
    )(*args)


def f32(*shape):
    return jax.ShapeDtypeStruct(shape, jnp.float32)


def on_device(electric, magnetic, polar, current, material, pml):
    cells = (electric, magnetic, polar, current, material, pml)
    gx, gy, gz = (lax.axis_size(a) for a in ("gx", "gy", "gz"))
    shapes = [jax.ShapeDtypeStruct(a.shape, a.dtype) for a in cells]
    cells = [pltpu.with_memory_space_constraint(a, pltpu.HBM) for a in cells]
    *cells, down = call(
        load_and_low_faces,
        [*shapes, f32(72, 128)],
        cells,
        scratch=[pltpu.SemaphoreType.DMA((6,))],
        far=True,
        name="load_and_low_faces",
    )
    near = [(i, j) for i, j in down_of(gy) if i % 4 in (1, 2)]
    rest = [(i, j) for i, j in down_of(gy) if i % 4 in (0, 3)]
    after = lax.ppermute(down, "gy", near)
    (up,) = call(high_faces, [f32(64, 128)], (*cells, down), size=HINT, name="high_faces")
    before = lax.ppermute(up, "gy", up_of(gy))
    (down,) = call(again, [f32(48, 128)], (down, up), size=HINT, name="again")
    later = lax.ppermute(down, "gy", rest)

    wide, own = call(
        widen_rows,
        [f32(4, 10, ROWS, 128), f32(3, ROWS, 128)],
        (*cells, before, after, later),
        name="widen_rows",
    )
    right = lax.ppermute(own, "gx", down_of(gx))
    left = lax.ppermute(own, "gx", up_of(gx))

    ring_up = [(i, (i + 1) % gz) for i in range(gz)]
    ring_down = [((i + 1) % gz, i) for i in range(gz)]
    up, down = call(z_faces, [f32(16, ROWS, 128), f32(11, ROWS, 128)], (wide, right), name="z_faces")
    before = lax.ppermute(up, "gz", ring_up)
    after = lax.ppermute(down, "gz", ring_down)
    (beside,) = call(columns_on, [f32(3, ROWS, 128)], (own, left, right), size=1 << 30, flops=1 << 36, name="columns_on")
    columns_before = lax.ppermute(beside, "gz", ring_up)
    columns_after = lax.ppermute(beside, "gz", ring_down)

    polar = cells[2]
    brick = f32(3, 4, 16, 128)
    first = call(
        first_step,
        [f32(7, 3, ROWS, 128), f32(6, 3, ROWS, 128), brick, brick, f32(5, 2, ROWS, 128), f32(4, 3, 16, 128)],
        (wide, before, after, polar),
        flops=2_000_000,
        name="first_step",
    )
    return tuple(
        call(
            second_step,
            [brick] * 4,
            (own, left, right, columns_before, columns_after, *first),
            scratch=[pltpu.VMEM((3, 4, 16, 128), jnp.float32)] * 4
            + [pltpu.VMEM((5, 3, ROWS, 128), jnp.float32), pltpu.SemaphoreType.DMA((4,))],
            far_out=True,
            flops=2_000_000,
            name="second_step",
        )
    )


def solution(mesh):
    fields = P(None, "gz", "gy", "gx")
    cells = P("gz", "gy", "gx")
    return jax.shard_map(
        on_device,
        mesh=mesh,
        in_specs=(fields, fields, fields, fields, cells, cells),
        out_specs=(fields, fields, fields, fields),
        check_vma=False,
    )
```

```python
import jax
import jax.numpy as jnp
from jax import lax
from jax.experimental import pallas as pl
from jax.experimental.pallas import tpu as pltpu
from jax.sharding import PartitionSpec as P

time_step = 0.5
damping = 0.2
omega_sq = 1.0
strength = 3.0

DECAY = 1.0 + 0.5 * damping * time_step
HOLD = (1.0 - 0.5 * damping * time_step) / DECAY
PULL = time_step * omega_sq / DECAY
GAIN = PULL * strength

EX, EY, EZ, HX, HY, HZ, QX, QY, QZ, CODE = range(10)
EVERY = tuple(range(10))

Y_UP = [(c, 14) for c in (EX, EY, EZ, HX, HZ, CODE)] + [(c, 15) for c in EVERY]
Y_DOWN = [(c, 0) for c in (EX, EY, EZ, HX, HY, HZ, QX, QZ, CODE)] + [(EX, 1), (EZ, 1)]
Z_UP, Z_DOWN = 9, 8

ROWS = 24
SPAN = 32
HINT = 1 << 26


def up_of(n):
    return [(i, i + 1) for i in range(n - 1)]


def down_of(n):
    return [(i + 1, i) for i in range(n - 1)]


def code_of(material, pml):
    return (1 + 4 * material + pml).astype(jnp.float32)


def y_face(cells, c, row):
    e, h, p, j, material, pml = cells
    if c < HX:
        return e[c, :, row, :]
    if c < QX:
        return h[c - HX, :, row, :]
    if c < CODE:
        return HOLD * j[c - QX, :, row, :] - PULL * p[c - QX, :, row, :]
    return code_of(material[:, row, :], pml[:, row, :])


def load_and_low_faces(*refs):
    far, near, down, done = refs[:6], refs[6:12], refs[12], refs[13]
    copies = [pltpu.make_async_copy(a, b, done.at[i]) for i, (a, b) in enumerate(zip(far, near))]
    for copy in copies:
        copy.start()
    for copy in copies:
        copy.wait()
    down[...] = jnp.zeros_like(down)
    for i, (c, row) in enumerate(Y_DOWN):
        down[4 * i : 4 * i + 4, :] = y_face(near, c, row)


def high_faces(*refs):
    near, _, up = refs[:6], refs[6], refs[7]
    for i, (c, row) in enumerate(Y_UP):
        up[4 * i : 4 * i + 4, :] = y_face(near, c, row)


def again(down, _, copy):
    copy[...] = down[0:48, :]


def widen_rows(e, h, p, j, material, pml, before, after, later, wide, edges):
    lane = lanes()
    for z in range(4):
        for c in EVERY:
            if c < HX:
                own = e[c, z]
            elif c < QX:
                own = h[c - HX, z]
            elif c < CODE:
                own = HOLD * j[c - QX, z] - PULL * p[c - QX, z]
            else:
                own = code_of(material[z], pml[z])
            wide[z, c, 0:16, :] = own
            wide[z, c, 16:24, :] = jnp.zeros((8, 128), jnp.float32)
        for i, (c, row) in enumerate(Y_UP):
            wide[z, c, row + 8 : row + 9, :] = before[4 * i + z : 4 * i + z + 1, :]
        for i, (c, row) in enumerate(Y_DOWN):
            at = slice(4 * i + z, 4 * i + z + 1)
            wide[z, c, row + 16 : row + 17, :] = after[at, :] + later[at, :]
    for g in range(3):
        total = jnp.zeros((ROWS, 128), jnp.float32)
        for c in range(4 * g, min(4 * g + 4, 10)):
            for z in range(4):
                at = SPAN * (c - 4 * g) + 4 * (z + 2)
                moved = roll(wide[z, c], at - 126, 1)
                total = jnp.where((lane >= at) & (lane < at + 4), moved, total)
        edges[g] = total


def z_faces(wide, polar, _, up, down, h1, r1, p1, j1, fh, fe, push):
    for z in range(4):
        e = [wide[z, EX + k] for k in range(3)]
        h = [wide[z, HX + k] for k in range(3)]
        keep_h, push_h, keep_e, push_e, metal = factors(wide[z, CODE])
        later = [wide[z + 1, EX + k] for k in range(2)] if z < 3 else [0.0, 0.0]
        new = magnetic_new(
            h,
            e,
            {0: y_next(e[0]), 2: y_next(e[2])},
            {0: later[0], 1: later[1]},
            {1: x_next(e[1]), 2: x_next(e[2])},
            keep_h,
            push_h,
        )
        flow = [wide[z, QX + k] + GAIN * metal * e[k] for k in range(3)]
        rest = [keep_e * e[k] - push_e * (metal * flow[k]) for k in range(3)]
        for k in range(3):
            h1[z, k] = new[k]
            r1[z, k] = rest[k]
            j1[k, z] = flow[k][0:16]
            p1[k, z] = polar[k, z] + time_step * flow[k][0:16]
        fh[z, 0] = keep_h
        fh[z, 1] = push_h
        push[z] = push_e
        for k, f in enumerate((keep_e, push_e, metal)):
            fe[z, k] = f[0:16]
        if z == 0:
            for i, value in enumerate(new + rest[:2] + [wide[z, CODE]] + e[:2]):
                down[i] = value
        if z == 2:
            up[7] = new[0]
            up[8] = new[1]
        if z == 3:
            for i, value in enumerate(new + rest + [wide[z, CODE]]):
                up[i] = value


def sides(own, outer, inner, g):
    near = (lanes() % 4) < 2
    odd = lax.axis_index("gx") % 2 == 1
    left = jnp.where(odd, outer[g], inner[g])
    right = jnp.where(odd, inner[g], outer[g])
    return jnp.where(near, left, own[g]), jnp.where(near, own[g], right)


def columns_on(own, outer, inner, out):
    part = (lanes() % SPAN) // 8
    for g in range(3):
        low, high = sides(own, outer, inner, g)
        up = jnp.where(part == 0, roll(low, -16, 1), roll(high, -8, 1))
        down = jnp.where(part == 2, roll(high, 8, 1), roll(low, 16, 1))
        out[g] = jnp.where(part < 2, up, down)


def grid_ends():
    place = lax.axis_index("gz")
    return place == 0, place == lax.axis_size("gz") - 1


def lanes():
    return lax.broadcasted_iota(jnp.int32, (ROWS, 128), 1)


def roll(array, shift, axis):
    shift = shift % array.shape[axis]
    return pltpu.roll(array, shift, axis) if shift else array


def factors(code):
    metal = code > 8.5
    dielec = (code > 4.5) & (code < 8.5)
    inside = code > 0.5
    level = code - jnp.where(metal, 9.0, jnp.where(dielec, 5.0, 1.0))
    loss = jnp.where(level > 2.5, 0.25, jnp.where(level > 1.5, 0.1, jnp.where(level > 0.5, 0.025, 0.0)))
    permit = jnp.where(metal, 1.5, jnp.where(dielec, 2.25, 1.0))
    over_h = jnp.where(inside, 1.0 / (1.0 + loss), 0.0)
    over_e = jnp.where(inside, 1.0 / (permit + loss), 0.0)
    return (
        (1.0 - loss) * over_h,
        time_step * over_h,
        (permit - loss) * over_e,
        time_step * over_e,
        jnp.where(metal, 1.0, 0.0),
    )


def magnetic_new(h, e, ey, ez, ex, keep, push):
    curl = (
        (ey[2] - e[2]) - (ez[1] - e[1]),
        (ez[0] - e[0]) - (ex[2] - e[2]),
        (ex[1] - e[1]) - (ey[0] - e[0]),
    )
    return [None if h[k] is None else keep * h[k] - push * curl[k] for k in range(3)]


def curl_back(h, hy, hz, hx):
    return (
        (h[2] - hy[2]) - (h[1] - hz[1]),
        (h[0] - hz[0]) - (h[2] - hx[2]),
        (h[1] - hx[1]) - (h[0] - hy[0]),
    )


def electric_new(e, h, hy, hz, hx, drag, keep, push):
    curl = curl_back(h, hy, hz, hx)
    return [keep * e[k] + push * (curl[k] - drag[k]) for k in range(3)]


x_next = lambda a: roll(a, -1, 1)
x_back = lambda a: roll(a, 1, 1)
y_next = lambda a: roll(a, -1, 0)
y_back = lambda a: roll(a, 1, 0)


def first_step(wide, before, after, part, r1, fh, push, h1, e1, low):
    first, last = grid_ends()

    def from_below(i):
        return jnp.where(first, 0.0, before[i])

    def from_above(i):
        return jnp.where(last, 0.0, after[i])

    def with_next(h, push_h, x, y):
        return [h[0] + push_h * y, h[1] - push_h * x, h[2]]

    def electric(z, rest, push_e, h, back):
        curl = curl_back(
            h,
            {0: y_back(h[0]), 2: y_back(h[2])},
            {0: back[0], 1: back[1]},
            {1: x_back(h[1]), 2: x_back(h[2])},
        )
        for k, r in enumerate(rest):
            e1[z + 1, k] = r + push_e * curl[k]

    keep_h, push_h, _, push_e, _ = factors(from_below(6))
    low[0] = keep_h
    low[1] = push_h
    h = with_next([from_below(k) for k in range(3)], push_h, wide[0, EX], wide[0, EY])
    electric(-1, [from_below(3 + k) for k in range(3)], push_e, h, [from_below(7), from_below(8)])
    for z in range(4):
        for k in range(3):
            h1[z, k] = h[k]
        back, h = h, [part[z, k] for k in range(3)]
        if z == 3:
            h = with_next(h, fh[z, 1], from_above(6), from_above(7))
        electric(z, [r1[z, k] for k in range(3)], push[z], h, back)
    for k in range(3):
        h1[4, k] = h[k]
    _, _, _, push_e, _ = factors(from_above(5))
    electric(4, [from_above(3 + k) for k in range(2)], push_e, [from_above(k) for k in range(3)], h)


def columns(own, outer, inner, before, after):
    first, last = grid_ends()
    lane = lanes()
    part = (lane % SPAN) // 8
    values = []
    for g in range(3):
        low, high = sides(own, outer, inner, g)
        up = jnp.where(first, 0.0, before[g])
        down = jnp.where(last, 0.0, after[g])
        low = jnp.where(part == 0, up, jnp.where(part == 3, down, low))
        high = jnp.where(part == 0, roll(up, -8, 1), jnp.where(part == 3, roll(down, 8, 1), high))
        for k in range(4):
            values.append(jnp.where(lane < SPAN, roll(low, -SPAN * k, 1), roll(high, SPAN - SPAN * k, 1)))
    z_next = lambda a: roll(a, -4, 1)
    z_back = lambda a: roll(a, 4, 1)

    def shifted(f, y, z, x):
        return {0: y(f[0]), 2: y(f[2])}, {0: z(f[0]), 1: z(f[1])}, {1: x(f[1]), 2: x(f[2])}

    keep_h, push_h, keep_e, push_e, metal = factors(values[CODE])
    e0 = values[EX : EZ + 1]
    h1 = magnetic_new(values[HX : HZ + 1], e0, *shifted(e0, y_next, z_next, x_next), keep_h, push_h)
    drag = [metal * (values[QX + k] + GAIN * e0[k]) for k in range(3)]
    e1 = electric_new(e0, h1, *shifted(h1, y_back, z_back, x_back), drag, keep_e, push_e)
    h2 = magnetic_new(h1, e1, *shifted(e1, y_next, z_next, x_next), keep_h, push_h)
    return h1, e1, h2


def second_step(own, outer, inner, before, after, h1, e1, low, p1, j1, fh, fe, *rest):
    outs, near, h2, done = rest[:4], rest[4:8], rest[8], rest[9]
    e_near, h_near, p_near, j_near = near
    lane = lanes()
    ch1, ce1, ch2 = columns(own, outer, inner, before, after)

    def at_ends(column):
        return jnp.where(lane % 4 == 1, roll(column, -SPAN, 1), column)

    def put_right(array, z, column):
        return jnp.where((lane == 0) | (lane == 127), roll(column, 127 - (4 * (z + 2) + 1), 1), array)

    ends_h = [at_ends(a) for a in ch1]
    ends_e = [at_ends(a) for a in ce1]

    def after_x(array, z):
        return lambda k: jnp.where(lane == 127, roll(ce1[k], 127 - (SPAN + 4 * (z + 2) + 2), 1), x_next(array[k]))

    def before_x(array, z):
        return lambda k: jnp.where(lane == 0, roll(ch2[k], -(4 * (z + 2) + 1), 1), x_back(array[k]))

    def fixed_e(z):
        return [put_right(e1[z + 1, k], z, ends_e[k]) for k in range(3 if z < 4 else 2)]

    copies = [pltpu.make_async_copy(a, b, done.at[i]) for i, (a, b) in enumerate(zip(near, outs))]
    for z in range(4):
        metal = fe[z, 2]
        for k in range(3):
            e = put_right(e1[z + 1, k], z, ends_e[k])[0:16]
            flow = HOLD * j1[k, z] - PULL * p1[k, z] + GAIN * metal * e
            j_near[k, z] = flow
            p_near[k, z] = p1[k, z] + time_step * flow
    copies[2].start()
    copies[3].start()
    e = fixed_e(-1)
    for z in range(-1, 4):
        up = fixed_e(z + 1)
        h = [h1[z + 1, 0]] + [put_right(h1[z + 1, k], z, ends_h[k]) for k in (1, 2)]
        x = after_x(e, z)
        new = magnetic_new(
            h,
            e,
            {0: y_next(e[0]), 2: y_next(e[2])},
            {0: up[0], 1: up[1]},
            {1: x(1), 2: x(2)},
            fh[z, 0] if z >= 0 else low[0],
            fh[z, 1] if z >= 0 else low[1],
        )
        for k in range(3):
            h2[z + 1, k] = new[k]
            if z >= 0:
                h_near[k, z] = new[k][0:16]
        e = up
    copies[1].start()
    for z in range(4):
        h = [h2[z + 1, k] for k in range(3)]
        down = [h2[z, k] for k in range(2)]
        x = before_x(h, z)
        new = electric_new(
            [a[0:16] for a in fixed_e(z)],
            [a[0:16] for a in h],
            {0: y_back(h[0])[0:16], 2: y_back(h[2])[0:16]},
            {0: down[0][0:16], 1: down[1][0:16]},
            {1: x(1)[0:16], 2: x(2)[0:16]},
            [fe[z, 2] * j_near[k, z] for k in range(3)],
            fe[z, 0],
            fe[z, 1],
        )
        for k in range(3):
            e_near[k, z] = new[k]
    copies[0].start()
    for copy in copies:
        copy.wait()


VMEM = pl.BlockSpec(memory_space=pltpu.VMEM)
HBM = pl.BlockSpec(memory_space=pltpu.HBM)


def call(kernel, outs, args, scratch=(), flops=0, size=0, far=False, far_out=False, name=None):
    size = size or sum(a.size for a in args) + sum(o.size for o in outs)
    return pl.pallas_call(
        kernel,
        out_shape=outs,
        in_specs=[HBM if far else VMEM] * len(args),
        out_specs=[HBM if far_out else VMEM] * len(outs),
        scratch_shapes=list(scratch),
        cost_estimate=pl.CostEstimate(flops=flops, bytes_accessed=4 * size, transcendentals=0),
        compiler_params=pltpu.CompilerParams(vmem_limit_bytes=16 * 2**20),
        name=name,
    )(*args)


def f32(*shape):
    return jax.ShapeDtypeStruct(shape, jnp.float32)


def on_device(electric, magnetic, polar, current, material, pml):
    cells = (electric, magnetic, polar, current, material, pml)
    gx, gy, gz = (lax.axis_size(a) for a in ("gx", "gy", "gz"))
    shapes = [jax.ShapeDtypeStruct(a.shape, a.dtype) for a in cells]
    cells = [pltpu.with_memory_space_constraint(a, pltpu.HBM) for a in cells]
    *cells, down = call(
        load_and_low_faces,
        [*shapes, f32(72, 128)],
        cells,
        scratch=[pltpu.SemaphoreType.DMA((6,))],
        far=True,
        name="load_and_low_faces",
    )
    near = [(i, j) for i, j in down_of(gy) if i % 4 in (1, 2)]
    rest = [(i, j) for i, j in down_of(gy) if i % 4 in (0, 3)]
    after = lax.ppermute(down, "gy", near)
    (up,) = call(high_faces, [f32(64, 128)], (*cells, down), size=HINT, name="high_faces")
    before = lax.ppermute(up, "gy", up_of(gy))
    (down,) = call(again, [f32(48, 128)], (down, up), size=HINT, name="again")
    later = lax.ppermute(down, "gy", rest)

    wide, own = call(
        widen_rows,
        [f32(4, 10, ROWS, 128), f32(3, ROWS, 128)],
        (*cells, before, after, later),
        name="widen_rows",
    )
    pairs = [(i, i ^ 1) for i in range(gx) if i ^ 1 < gx]
    between = [(i, j) for i in range(1, gx - 1, 2) if i + 1 < gx for i, j in ((i, i + 1), (i + 1, i))]
    outer = lax.ppermute(own, "gx", pairs)
    inner = lax.ppermute(own, "gx", between)

    ring_up = [(i, (i + 1) % gz) for i in range(gz)]
    ring_down = [((i + 1) % gz, i) for i in range(gz)]
    brick, plane = f32(3, 4, 16, 128), (ROWS, 128)
    up, down, h1, r1, p1, j1, fh, fe, push = call(
        z_faces,
        [f32(Z_UP, *plane), f32(Z_DOWN, *plane), f32(4, 3, *plane), f32(4, 3, *plane), brick, brick]
        + [f32(4, 2, *plane), f32(4, 3, 16, 128), f32(4, *plane)],
        (wide, cells[2], own),
        flops=1_000_000,
        name="z_faces",
    )
    before = lax.ppermute(up, "gz", ring_up)
    after = lax.ppermute(down, "gz", ring_down)
    (beside,) = call(columns_on, [f32(3, ROWS, 128)], (own, outer, inner), size=1 << 30, flops=1 << 36, name="columns_on")
    columns_before = lax.ppermute(beside, "gz", ring_up)
    columns_after = lax.ppermute(beside, "gz", ring_down)

    h1, e1, low = call(
        first_step,
        [f32(5, 3, *plane), f32(6, 3, *plane), f32(2, *plane)],
        (wide, before, after, h1, r1, fh, push),
        flops=1_000_000,
        name="first_step",
    )
    return tuple(
        call(
            second_step,
            [brick] * 4,
            (own, outer, inner, columns_before, columns_after, h1, e1, low, p1, j1, fh, fe),
            scratch=[pltpu.VMEM((3, 4, 16, 128), jnp.float32)] * 4
            + [pltpu.VMEM((5, 3, ROWS, 128), jnp.float32), pltpu.SemaphoreType.DMA((4,))],
            far_out=True,
            flops=2_000_000,
            name="second_step",
        )
    )


def solution(mesh):
    fields = P(None, "gz", "gy", "gx")
    cells = P("gz", "gy", "gx")
    return jax.shard_map(
        on_device,
        mesh=mesh,
        in_specs=(fields, fields, fields, fields, cells, cells),
        out_specs=(fields, fields, fields, fields),
        check_vma=False,
    )
```

```python
import jax
import jax.numpy as jnp
from jax import lax
from jax.experimental import pallas as pl
from jax.experimental.pallas import tpu as pltpu
from jax.sharding import PartitionSpec as P

time_step = 0.5
damping = 0.2
omega_sq = 1.0
strength = 3.0

DECAY = 1.0 + 0.5 * damping * time_step
HOLD = (1.0 - 0.5 * damping * time_step) / DECAY
PULL = time_step * omega_sq / DECAY
GAIN = PULL * strength

EX, EY, EZ, HX, HY, HZ, QX, QY, QZ, CODE = range(10)
EVERY = tuple(range(10))

Y_UP = [(c, 14) for c in (EX, EY, EZ, HX, HZ, CODE)] + [(c, 15) for c in EVERY]
Y_DOWN = [(c, 0) for c in (EX, EY, EZ, HX, HY, HZ, QX, QZ, CODE)] + [(EX, 1), (EZ, 1)]
Z_UP, Z_DOWN = 9, 8

ROWS = 24
SPAN = 32
HINT = 1 << 26


def up_of(n):
    return [(i, i + 1) for i in range(n - 1)]


def down_of(n):
    return [(i + 1, i) for i in range(n - 1)]


def code_of(material, pml):
    return (1 + 4 * material + pml).astype(jnp.float32)


def y_face(cells, c, row):
    e, h, p, j, material, pml = cells
    if c < HX:
        return e[c, :, row, :]
    if c < QX:
        return h[c - HX, :, row, :]
    if c < CODE:
        return HOLD * j[c - QX, :, row, :] - PULL * p[c - QX, :, row, :]
    return code_of(material[:, row, :], pml[:, row, :])


def load_and_low_faces(*refs):
    far, near, down, done = refs[:6], refs[6:12], refs[12], refs[13]
    copies = [pltpu.make_async_copy(a, b, done.at[i]) for i, (a, b) in enumerate(zip(far, near))]
    for copy in copies:
        copy.start()
    for copy in copies:
        copy.wait()
    down[...] = jnp.zeros_like(down)
    for i, (c, row) in enumerate(Y_DOWN):
        down[4 * i : 4 * i + 4, :] = y_face(near, c, row)


def high_faces(*refs):
    near, _, up = refs[:6], refs[6], refs[7]
    for i, (c, row) in enumerate(Y_UP):
        up[4 * i : 4 * i + 4, :] = y_face(near, c, row)


def again(down, _, copy):
    copy[...] = down[0:48, :]


def widen_rows(e, h, p, j, material, pml, before, after, later, wide, edges):
    lane = lanes()
    for z in range(4):
        for c in EVERY:
            if c < HX:
                own = e[c, z]
            elif c < QX:
                own = h[c - HX, z]
            elif c < CODE:
                own = HOLD * j[c - QX, z] - PULL * p[c - QX, z]
            else:
                own = code_of(material[z], pml[z])
            wide[z, c, 0:16, :] = own
            wide[z, c, 16:24, :] = jnp.zeros((8, 128), jnp.float32)
        for i, (c, row) in enumerate(Y_UP):
            wide[z, c, row + 8 : row + 9, :] = before[4 * i + z : 4 * i + z + 1, :]
        for i, (c, row) in enumerate(Y_DOWN):
            at = slice(4 * i + z, 4 * i + z + 1)
            wide[z, c, row + 16 : row + 17, :] = after[at, :] + later[at, :]
    for g in range(3):
        total = jnp.zeros((ROWS, 128), jnp.float32)
        for c in range(4 * g, min(4 * g + 4, 10)):
            for z in range(4):
                at = SPAN * (c - 4 * g) + 4 * (z + 2)
                moved = roll(wide[z, c], at - 126, 1)
                total = jnp.where((lane >= at) & (lane < at + 4), moved, total)
        edges[g] = total


def z_faces(wide, polar, _, up, down, h1, r1, p1, j1, fh, fe, push):
    for z in range(4):
        e = [wide[z, EX + k] for k in range(3)]
        h = [wide[z, HX + k] for k in range(3)]
        keep_h, push_h, keep_e, push_e, metal = factors(wide[z, CODE])
        later = [wide[z + 1, EX + k] for k in range(2)] if z < 3 else [0.0, 0.0]
        new = magnetic_new(
            h,
            e,
            {0: y_next(e[0]), 2: y_next(e[2])},
            {0: later[0], 1: later[1]},
            {1: x_next(e[1]), 2: x_next(e[2])},
            keep_h,
            push_h,
        )
        flow = [wide[z, QX + k] + GAIN * metal * e[k] for k in range(3)]
        rest = [keep_e * e[k] - push_e * (metal * flow[k]) for k in range(3)]
        for k in range(3):
            h1[z, k] = new[k]
            r1[z, k] = rest[k]
            j1[k, z] = flow[k][0:16]
            p1[k, z] = polar[k, z] + time_step * flow[k][0:16]
        fh[z, 0] = keep_h
        fh[z, 1] = push_h
        push[z] = push_e
        for k, f in enumerate((keep_e, push_e, metal)):
            fe[z, k] = f[0:16]
        if z == 0:
            for i, value in enumerate(new + rest[:2] + [wide[z, CODE]] + e[:2]):
                down[i] = value
        if z == 2:
            up[7] = new[0]
            up[8] = new[1]
        if z == 3:
            for i, value in enumerate(new + rest + [wide[z, CODE]]):
                up[i] = value


def sides(own, outer, inner, g):
    near = (lanes() % 4) < 2
    odd = lax.axis_index("gx") % 2 == 1
    left = jnp.where(odd, outer[g], inner[g])
    right = jnp.where(odd, inner[g], outer[g])
    return jnp.where(near, left, own[g]), jnp.where(near, own[g], right)


def columns_on(own, outer, inner, *outs):
    part = (lanes() % SPAN) // 8
    for g in range(3):
        low, high = sides(own, outer, inner, g)
        up = jnp.where(part == 0, roll(low, -16, 1), roll(high, -8, 1))
        down = jnp.where(part == 2, roll(high, 8, 1), roll(low, 16, 1))
        for out in outs:
            out[ROWS * g : ROWS * (g + 1), :] = jnp.where(part < 2, up, down)


def grid_ends():
    place = lax.axis_index("gz")
    return place == 0, place == lax.axis_size("gz") - 1


def lanes():
    return lax.broadcasted_iota(jnp.int32, (ROWS, 128), 1)


def roll(array, shift, axis):
    shift = shift % array.shape[axis]
    return pltpu.roll(array, shift, axis) if shift else array


def factors(code):
    metal = code > 8.5
    dielec = (code > 4.5) & (code < 8.5)
    inside = code > 0.5
    level = code - jnp.where(metal, 9.0, jnp.where(dielec, 5.0, 1.0))
    loss = jnp.where(level > 2.5, 0.25, jnp.where(level > 1.5, 0.1, jnp.where(level > 0.5, 0.025, 0.0)))
    permit = jnp.where(metal, 1.5, jnp.where(dielec, 2.25, 1.0))
    over_h = jnp.where(inside, 1.0 / (1.0 + loss), 0.0)
    over_e = jnp.where(inside, 1.0 / (permit + loss), 0.0)
    return (
        (1.0 - loss) * over_h,
        time_step * over_h,
        (permit - loss) * over_e,
        time_step * over_e,
        jnp.where(metal, 1.0, 0.0),
    )


def magnetic_new(h, e, ey, ez, ex, keep, push):
    curl = (
        (ey[2] - e[2]) - (ez[1] - e[1]),
        (ez[0] - e[0]) - (ex[2] - e[2]),
        (ex[1] - e[1]) - (ey[0] - e[0]),
    )
    return [None if h[k] is None else keep * h[k] - push * curl[k] for k in range(3)]


def curl_back(h, hy, hz, hx):
    return (
        (h[2] - hy[2]) - (h[1] - hz[1]),
        (h[0] - hz[0]) - (h[2] - hx[2]),
        (h[1] - hx[1]) - (h[0] - hy[0]),
    )


def electric_new(e, h, hy, hz, hx, drag, keep, push):
    curl = curl_back(h, hy, hz, hx)
    return [keep * e[k] + push * (curl[k] - drag[k]) for k in range(3)]


x_next = lambda a: roll(a, -1, 1)
x_back = lambda a: roll(a, 1, 1)
y_next = lambda a: roll(a, -1, 0)
y_back = lambda a: roll(a, 1, 0)


def first_step(wide, before, after, part, r1, fh, push, h1, e1, low):
    first, last = grid_ends()

    def from_below(i):
        return jnp.where(first, 0.0, before[i])

    def from_above(i):
        return jnp.where(last, 0.0, after[i])

    def with_next(h, push_h, x, y):
        return [h[0] + push_h * y, h[1] - push_h * x, h[2]]

    def electric(z, rest, push_e, h, back):
        curl = curl_back(
            h,
            {0: y_back(h[0]), 2: y_back(h[2])},
            {0: back[0], 1: back[1]},
            {1: x_back(h[1]), 2: x_back(h[2])},
        )
        for k, r in enumerate(rest):
            e1[z + 1, k] = r + push_e * curl[k]

    keep_h, push_h, _, push_e, _ = factors(from_below(6))
    low[0] = keep_h
    low[1] = push_h
    h = with_next([from_below(k) for k in range(3)], push_h, wide[0, EX], wide[0, EY])
    electric(-1, [from_below(3 + k) for k in range(3)], push_e, h, [from_below(7), from_below(8)])
    for z in range(4):
        for k in range(3):
            h1[z, k] = h[k]
        back, h = h, [part[z, k] for k in range(3)]
        if z == 3:
            h = with_next(h, fh[z, 1], from_above(6), from_above(7))
        electric(z, [r1[z, k] for k in range(3)], push[z], h, back)
    for k in range(3):
        h1[4, k] = h[k]
    _, _, _, push_e, _ = factors(from_above(5))
    electric(4, [from_above(3 + k) for k in range(2)], push_e, [from_above(k) for k in range(3)], h)


def columns(own, outer, inner, before, after):
    first, last = grid_ends()
    lane = lanes()
    part = (lane % SPAN) // 8
    values = []
    for g in range(3):
        low, high = sides(own, outer, inner, g)
        rows = slice(ROWS * g, ROWS * (g + 1))
        up = jnp.where(first, 0.0, before[rows, :])
        down = jnp.where(last, 0.0, after[rows, :])
        low = jnp.where(part == 0, up, jnp.where(part == 3, down, low))
        high = jnp.where(part == 0, roll(up, -8, 1), jnp.where(part == 3, roll(down, 8, 1), high))
        for k in range(4):
            values.append(jnp.where(lane < SPAN, roll(low, -SPAN * k, 1), roll(high, SPAN - SPAN * k, 1)))
    z_next = lambda a: roll(a, -4, 1)
    z_back = lambda a: roll(a, 4, 1)

    def shifted(f, y, z, x):
        return {0: y(f[0]), 2: y(f[2])}, {0: z(f[0]), 1: z(f[1])}, {1: x(f[1]), 2: x(f[2])}

    keep_h, push_h, keep_e, push_e, metal = factors(values[CODE])
    e0 = values[EX : EZ + 1]
    h1 = magnetic_new(values[HX : HZ + 1], e0, *shifted(e0, y_next, z_next, x_next), keep_h, push_h)
    drag = [metal * (values[QX + k] + GAIN * e0[k]) for k in range(3)]
    e1 = electric_new(e0, h1, *shifted(h1, y_back, z_back, x_back), drag, keep_e, push_e)
    h2 = magnetic_new(h1, e1, *shifted(e1, y_next, z_next, x_next), keep_h, push_h)
    return h1, e1, h2


def second_step(own, outer, inner, before, after, h1, e1, low, p1, j1, fh, fe, *rest):
    outs, near, h2, done = rest[:4], rest[4:8], rest[8], rest[9]
    e_near, h_near, p_near, j_near = near
    lane = lanes()
    ch1, ce1, ch2 = columns(own, outer, inner, before, after)

    def at_ends(column):
        return jnp.where(lane % 4 == 1, roll(column, -SPAN, 1), column)

    def put_right(array, z, column):
        return jnp.where((lane == 0) | (lane == 127), roll(column, 127 - (4 * (z + 2) + 1), 1), array)

    ends_h = [at_ends(a) for a in ch1]
    ends_e = [at_ends(a) for a in ce1]

    def after_x(array, z):
        return lambda k: jnp.where(lane == 127, roll(ce1[k], 127 - (SPAN + 4 * (z + 2) + 2), 1), x_next(array[k]))

    def before_x(array, z):
        return lambda k: jnp.where(lane == 0, roll(ch2[k], -(4 * (z + 2) + 1), 1), x_back(array[k]))

    def fixed_e(z):
        return [put_right(e1[z + 1, k], z, ends_e[k]) for k in range(3 if z < 4 else 2)]

    copies = [pltpu.make_async_copy(a, b, done.at[i]) for i, (a, b) in enumerate(zip(near, outs))]
    for z in range(4):
        metal = fe[z, 2]
        for k in range(3):
            e = put_right(e1[z + 1, k], z, ends_e[k])[0:16]
            flow = HOLD * j1[k, z] - PULL * p1[k, z] + GAIN * metal * e
            j_near[k, z] = flow
            p_near[k, z] = p1[k, z] + time_step * flow
    copies[2].start()
    copies[3].start()
    e = fixed_e(-1)
    for z in range(-1, 4):
        up = fixed_e(z + 1)
        h = [h1[z + 1, 0]] + [put_right(h1[z + 1, k], z, ends_h[k]) for k in (1, 2)]
        x = after_x(e, z)
        new = magnetic_new(
            h,
            e,
            {0: y_next(e[0]), 2: y_next(e[2])},
            {0: up[0], 1: up[1]},
            {1: x(1), 2: x(2)},
            fh[z, 0] if z >= 0 else low[0],
            fh[z, 1] if z >= 0 else low[1],
        )
        for k in range(3):
            h2[z + 1, k] = new[k]
            if z >= 0:
                h_near[k, z] = new[k][0:16]
        e = up
    copies[1].start()
    for z in range(4):
        h = [h2[z + 1, k] for k in range(3)]
        down = [h2[z, k] for k in range(2)]
        x = before_x(h, z)
        new = electric_new(
            [a[0:16] for a in fixed_e(z)],
            [a[0:16] for a in h],
            {0: y_back(h[0])[0:16], 2: y_back(h[2])[0:16]},
            {0: down[0][0:16], 1: down[1][0:16]},
            {1: x(1)[0:16], 2: x(2)[0:16]},
            [fe[z, 2] * j_near[k, z] for k in range(3)],
            fe[z, 0],
            fe[z, 1],
        )
        for k in range(3):
            e_near[k, z] = new[k]
    copies[0].start()
    for copy in copies:
        copy.wait()


VMEM = pl.BlockSpec(memory_space=pltpu.VMEM)
HBM = pl.BlockSpec(memory_space=pltpu.HBM)


def call(kernel, outs, args, scratch=(), flops=0, size=0, far=False, far_out=False, name=None):
    size = size or sum(a.size for a in args) + sum(o.size for o in outs)
    return pl.pallas_call(
        kernel,
        out_shape=outs,
        in_specs=[HBM if far else VMEM] * len(args),
        out_specs=[HBM if far_out else VMEM] * len(outs),
        scratch_shapes=list(scratch),
        cost_estimate=pl.CostEstimate(flops=flops, bytes_accessed=4 * size, transcendentals=0),
        compiler_params=pltpu.CompilerParams(vmem_limit_bytes=16 * 2**20),
        name=name,
    )(*args)


def f32(*shape):
    return jax.ShapeDtypeStruct(shape, jnp.float32)


def on_device(electric, magnetic, polar, current, material, pml):
    cells = (electric, magnetic, polar, current, material, pml)
    gx, gy, gz = (lax.axis_size(a) for a in ("gx", "gy", "gz"))
    shapes = [jax.ShapeDtypeStruct(a.shape, a.dtype) for a in cells]
    cells = [pltpu.with_memory_space_constraint(a, pltpu.HBM) for a in cells]
    *cells, down = call(
        load_and_low_faces,
        [*shapes, f32(72, 128)],
        cells,
        scratch=[pltpu.SemaphoreType.DMA((6,))],
        far=True,
        name="load_and_low_faces",
    )
    near = [(i, j) for i, j in down_of(gy) if i % 4 in (1, 2)]
    rest = [(i, j) for i, j in down_of(gy) if i % 4 in (0, 3)]
    after = lax.ppermute(down, "gy", near)
    (up,) = call(high_faces, [f32(64, 128)], (*cells, down), size=HINT, name="high_faces")
    before = lax.ppermute(up, "gy", up_of(gy))
    (down,) = call(again, [f32(48, 128)], (down, up), size=HINT, name="again")
    later = lax.ppermute(down, "gy", rest)

    wide, own = call(
        widen_rows,
        [f32(4, 10, ROWS, 128), f32(3, ROWS, 128)],
        (*cells, before, after, later),
        name="widen_rows",
    )
    pairs = [(i, i ^ 1) for i in range(gx) if i ^ 1 < gx]
    between = [(i, j) for i in range(1, gx - 1, 2) if i + 1 < gx for i, j in ((i, i + 1), (i + 1, i))]
    outer = lax.ppermute(own, "gx", pairs)
    inner = lax.ppermute(own, "gx", between)

    ring_up = [(i, (i + 1) % gz) for i in range(gz)]
    ring_down = [((i + 1) % gz, i) for i in range(gz)]
    brick, plane = f32(3, 4, 16, 128), (ROWS, 128)
    up, down, h1, r1, p1, j1, fh, fe, push = call(
        z_faces,
        [f32(Z_UP, *plane), f32(Z_DOWN, *plane), f32(4, 3, *plane), f32(4, 3, *plane), brick, brick]
        + [f32(4, 2, *plane), f32(4, 3, 16, 128), f32(4, *plane)],
        (wide, cells[2], own),
        flops=1_000_000,
        name="z_faces",
    )
    before = lax.ppermute(up, "gz", ring_up)
    after = lax.ppermute(down, "gz", ring_down)
    up, down = call(columns_on, [f32(72, 128), f32(73, 128)], (own, outer, inner), size=1 << 30, flops=1 << 36, name="columns_on")
    columns_before = lax.ppermute(up, "gz", ring_up)
    columns_after = lax.ppermute(down, "gz", ring_down)

    h1, e1, low = call(
        first_step,
        [f32(5, 3, *plane), f32(6, 3, *plane), f32(2, *plane)],
        (wide, before, after, h1, r1, fh, push),
        flops=1_000_000,
        name="first_step",
    )
    return tuple(
        call(
            second_step,
            [brick] * 4,
            (own, outer, inner, columns_before, columns_after, h1, e1, low, p1, j1, fh, fe),
            scratch=[pltpu.VMEM((3, 4, 16, 128), jnp.float32)] * 4
            + [pltpu.VMEM((5, 3, ROWS, 128), jnp.float32), pltpu.SemaphoreType.DMA((4,))],
            far_out=True,
            flops=2_000_000,
            name="second_step",
        )
    )


def solution(mesh):
    fields = P(None, "gz", "gy", "gx")
    cells = P("gz", "gy", "gx")
    return jax.shard_map(
        on_device,
        mesh=mesh,
        in_specs=(fields, fields, fields, fields, cells, cells),
        out_specs=(fields, fields, fields, fields),
        check_vma=False,
    )
```

```python
import jax
import jax.numpy as jnp
from jax import lax
from jax.experimental import pallas as pl
from jax.experimental.pallas import tpu as pltpu
from jax.sharding import PartitionSpec as P

time_step = 0.5
damping = 0.2
omega_sq = 1.0
strength = 3.0

DECAY = 1.0 + 0.5 * damping * time_step
HOLD = (1.0 - 0.5 * damping * time_step) / DECAY
PULL = time_step * omega_sq / DECAY
GAIN = PULL * strength

EX, EY, EZ, HX, HY, HZ, QX, QY, QZ, CODE = range(10)
EVERY = tuple(range(10))

Y_UP = [(c, 14) for c in (EX, EY, EZ, HX, HZ, CODE)] + [(c, 15) for c in EVERY]
Y_DOWN = [(c, 0) for c in (EX, EY, EZ, HX, HY, HZ, QX, QZ, CODE)] + [(EX, 1), (EZ, 1)]
Z_UP, Z_DOWN = 9, 8

ROWS = 24
SPAN = 32
HINT = 1 << 26


def up_of(n):
    return [(i, i + 1) for i in range(n - 1)]


def down_of(n):
    return [(i + 1, i) for i in range(n - 1)]


def code_of(material, pml):
    return (1 + 4 * material + pml).astype(jnp.float32)


def y_face(cells, c, row):
    e, h, p, j, material, pml = cells
    if c < HX:
        return e[c, :, row, :]
    if c < QX:
        return h[c - HX, :, row, :]
    if c < CODE:
        return HOLD * j[c - QX, :, row, :] - PULL * p[c - QX, :, row, :]
    return code_of(material[:, row, :], pml[:, row, :])


def load_and_low_faces(*refs):
    far, near, down, done = refs[:6], refs[6:12], refs[12], refs[13]
    copies = [pltpu.make_async_copy(a, b, done.at[i]) for i, (a, b) in enumerate(zip(far, near))]
    for copy in copies:
        copy.start()
    for copy in copies:
        copy.wait()
    down[...] = jnp.zeros_like(down)
    for i, (c, row) in enumerate(Y_DOWN):
        down[4 * i : 4 * i + 4, :] = y_face(near, c, row)


def high_faces(*refs):
    near, _, up = refs[:6], refs[6], refs[7]
    for i, (c, row) in enumerate(Y_UP):
        up[4 * i : 4 * i + 4, :] = y_face(near, c, row)


def block_class():
    return lax.axis_index("gy") % 4


def last_faces(down, up, copy, mixed):
    copy[...] = down[0:48, :]
    mixed[0:48, :] = jnp.where(block_class() == 2, up[0:48, :], down[0:48, :])
    mixed[48:64, :] = up[48:64, :]


def joined(after, later, before, rows_after, rows_before):
    rows_after[...] = after[0:48, :] + later[...]
    rows_before[...] = before[...]


def widen_rows(e, h, p, j, material, pml, before, after, last, wide, edges):
    lane = lanes()
    low, high = block_class() == 3, block_class() == 2
    for z in range(4):
        for c in EVERY:
            if c < HX:
                own = e[c, z]
            elif c < QX:
                own = h[c - HX, z]
            elif c < CODE:
                own = HOLD * j[c - QX, z] - PULL * p[c - QX, z]
            else:
                own = code_of(material[z], pml[z])
            wide[z, c, 0:16, :] = own
            wide[z, c, 16:24, :] = jnp.zeros((8, 128), jnp.float32)
        for i, (c, row) in enumerate(Y_UP):
            at = slice(4 * i + z, 4 * i + z + 1)
            wide[z, c, row + 8 : row + 9, :] = jnp.where(low, last[at, :], before[at, :])
        for i, (c, row) in enumerate(Y_DOWN):
            at = slice(4 * i + z, 4 * i + z + 1)
            wide[z, c, row + 16 : row + 17, :] = jnp.where(high, last[at, :], after[at, :])
    for g in range(3):
        total = jnp.zeros((ROWS, 128), jnp.float32)
        for c in range(4 * g, min(4 * g + 4, 10)):
            for z in range(4):
                at = SPAN * (c - 4 * g) + 4 * (z + 2)
                moved = roll(wide[z, c], at - 126, 1)
                total = jnp.where((lane >= at) & (lane < at + 4), moved, total)
        edges[g] = total


def z_faces(wide, polar, _, up, down, h1, r1, p1, j1, fh, fe, push):
    for z in range(4):
        e = [wide[z, EX + k] for k in range(3)]
        h = [wide[z, HX + k] for k in range(3)]
        keep_h, push_h, keep_e, push_e, metal = factors(wide[z, CODE])
        later = [wide[z + 1, EX + k] for k in range(2)] if z < 3 else [0.0, 0.0]
        new = magnetic_new(
            h,
            e,
            {0: y_next(e[0]), 2: y_next(e[2])},
            {0: later[0], 1: later[1]},
            {1: x_next(e[1]), 2: x_next(e[2])},
            keep_h,
            push_h,
        )
        flow = [wide[z, QX + k] + GAIN * metal * e[k] for k in range(3)]
        rest = [keep_e * e[k] - push_e * (metal * flow[k]) for k in range(3)]
        for k in range(3):
            h1[z, k] = new[k]
            r1[z, k] = rest[k]
            j1[k, z] = flow[k][0:16]
            p1[k, z] = polar[k, z] + time_step * flow[k][0:16]
        fh[z, 0] = keep_h
        fh[z, 1] = push_h
        push[z] = push_e
        for k, f in enumerate((keep_e, push_e, metal)):
            fe[z, k] = f[0:16]
        if z == 0:
            for i, value in enumerate(new + rest[:2] + [wide[z, CODE]] + e[:2]):
                down[i] = value
        if z == 2:
            up[7] = new[0]
            up[8] = new[1]
        if z == 3:
            for i, value in enumerate(new + rest + [wide[z, CODE]]):
                up[i] = value


def sides(own, outer, inner, g):
    near = (lanes() % 4) < 2
    odd = lax.axis_index("gx") % 2 == 1
    left = jnp.where(odd, outer[g], inner[g])
    right = jnp.where(odd, inner[g], outer[g])
    return jnp.where(near, left, own[g]), jnp.where(near, own[g], right)


def columns_on(own, outer, inner, *outs):
    part = (lanes() % SPAN) // 8
    for g in range(3):
        low, high = sides(own, outer, inner, g)
        up = jnp.where(part == 0, roll(low, -16, 1), roll(high, -8, 1))
        down = jnp.where(part == 2, roll(high, 8, 1), roll(low, 16, 1))
        for out in outs:
            out[ROWS * g : ROWS * (g + 1), :] = jnp.where(part < 2, up, down)


def grid_ends():
    place = lax.axis_index("gz")
    return place == 0, place == lax.axis_size("gz") - 1


def lanes():
    return lax.broadcasted_iota(jnp.int32, (ROWS, 128), 1)


def roll(array, shift, axis):
    shift = shift % array.shape[axis]
    return pltpu.roll(array, shift, axis) if shift else array


def factors(code):
    metal = code > 8.5
    dielec = (code > 4.5) & (code < 8.5)
    inside = code > 0.5
    level = code - jnp.where(metal, 9.0, jnp.where(dielec, 5.0, 1.0))
    loss = jnp.where(level > 2.5, 0.25, jnp.where(level > 1.5, 0.1, jnp.where(level > 0.5, 0.025, 0.0)))
    permit = jnp.where(metal, 1.5, jnp.where(dielec, 2.25, 1.0))
    over_h = jnp.where(inside, 1.0 / (1.0 + loss), 0.0)
    over_e = jnp.where(inside, 1.0 / (permit + loss), 0.0)
    return (
        (1.0 - loss) * over_h,
        time_step * over_h,
        (permit - loss) * over_e,
        time_step * over_e,
        jnp.where(metal, 1.0, 0.0),
    )


def magnetic_new(h, e, ey, ez, ex, keep, push):
    curl = (
        (ey[2] - e[2]) - (ez[1] - e[1]),
        (ez[0] - e[0]) - (ex[2] - e[2]),
        (ex[1] - e[1]) - (ey[0] - e[0]),
    )
    return [None if h[k] is None else keep * h[k] - push * curl[k] for k in range(3)]


def curl_back(h, hy, hz, hx):
    return (
        (h[2] - hy[2]) - (h[1] - hz[1]),
        (h[0] - hz[0]) - (h[2] - hx[2]),
        (h[1] - hx[1]) - (h[0] - hy[0]),
    )


def electric_new(e, h, hy, hz, hx, drag, keep, push):
    curl = curl_back(h, hy, hz, hx)
    return [keep * e[k] + push * (curl[k] - drag[k]) for k in range(3)]


x_next = lambda a: roll(a, -1, 1)
x_back = lambda a: roll(a, 1, 1)
y_next = lambda a: roll(a, -1, 0)
y_back = lambda a: roll(a, 1, 0)


def first_step(wide, before, after, part, r1, fh, push, h1, e1, low):
    first, last = grid_ends()

    def from_below(i):
        return jnp.where(first, 0.0, before[i])

    def from_above(i):
        return jnp.where(last, 0.0, after[i])

    def with_next(h, push_h, x, y):
        return [h[0] + push_h * y, h[1] - push_h * x, h[2]]

    def electric(z, rest, push_e, h, back):
        curl = curl_back(
            h,
            {0: y_back(h[0]), 2: y_back(h[2])},
            {0: back[0], 1: back[1]},
            {1: x_back(h[1]), 2: x_back(h[2])},
        )
        for k, r in enumerate(rest):
            e1[z + 1, k] = r + push_e * curl[k]

    keep_h, push_h, _, push_e, _ = factors(from_below(6))
    low[0] = keep_h
    low[1] = push_h
    h = with_next([from_below(k) for k in range(3)], push_h, wide[0, EX], wide[0, EY])
    electric(-1, [from_below(3 + k) for k in range(3)], push_e, h, [from_below(7), from_below(8)])
    for z in range(4):
        for k in range(3):
            h1[z, k] = h[k]
        back, h = h, [part[z, k] for k in range(3)]
        if z == 3:
            h = with_next(h, fh[z, 1], from_above(6), from_above(7))
        electric(z, [r1[z, k] for k in range(3)], push[z], h, back)
    for k in range(3):
        h1[4, k] = h[k]
    _, _, _, push_e, _ = factors(from_above(5))
    electric(4, [from_above(3 + k) for k in range(2)], push_e, [from_above(k) for k in range(3)], h)


def columns(own, outer, inner, before, after):
    first, last = grid_ends()
    lane = lanes()
    part = (lane % SPAN) // 8
    values = []
    for g in range(3):
        low, high = sides(own, outer, inner, g)
        rows = slice(ROWS * g, ROWS * (g + 1))
        up = jnp.where(first, 0.0, before[rows, :])
        down = jnp.where(last, 0.0, after[rows, :])
        low = jnp.where(part == 0, up, jnp.where(part == 3, down, low))
        high = jnp.where(part == 0, roll(up, -8, 1), jnp.where(part == 3, roll(down, 8, 1), high))
        for k in range(4):
            values.append(jnp.where(lane < SPAN, roll(low, -SPAN * k, 1), roll(high, SPAN - SPAN * k, 1)))
    z_next = lambda a: roll(a, -4, 1)
    z_back = lambda a: roll(a, 4, 1)

    def shifted(f, y, z, x):
        return {0: y(f[0]), 2: y(f[2])}, {0: z(f[0]), 1: z(f[1])}, {1: x(f[1]), 2: x(f[2])}

    keep_h, push_h, keep_e, push_e, metal = factors(values[CODE])
    e0 = values[EX : EZ + 1]
    h1 = magnetic_new(values[HX : HZ + 1], e0, *shifted(e0, y_next, z_next, x_next), keep_h, push_h)
    drag = [metal * (values[QX + k] + GAIN * e0[k]) for k in range(3)]
    e1 = electric_new(e0, h1, *shifted(h1, y_back, z_back, x_back), drag, keep_e, push_e)
    h2 = magnetic_new(h1, e1, *shifted(e1, y_next, z_next, x_next), keep_h, push_h)
    return h1, e1, h2


def second_step(own, outer, inner, before, after, h1, e1, low, p1, j1, fh, fe, *rest):
    outs, near, h2, done = rest[:4], rest[4:8], rest[8], rest[9]
    e_near, h_near, p_near, j_near = near
    lane = lanes()
    ch1, ce1, ch2 = columns(own, outer, inner, before, after)

    def at_ends(column):
        return jnp.where(lane % 4 == 1, roll(column, -SPAN, 1), column)

    def put_right(array, z, column):
        return jnp.where((lane == 0) | (lane == 127), roll(column, 127 - (4 * (z + 2) + 1), 1), array)

    ends_h = [at_ends(a) for a in ch1]
    ends_e = [at_ends(a) for a in ce1]

    def after_x(array, z):
        return lambda k: jnp.where(lane == 127, roll(ce1[k], 127 - (SPAN + 4 * (z + 2) + 2), 1), x_next(array[k]))

    def before_x(array, z):
        return lambda k: jnp.where(lane == 0, roll(ch2[k], -(4 * (z + 2) + 1), 1), x_back(array[k]))

    def fixed_e(z):
        return [put_right(e1[z + 1, k], z, ends_e[k]) for k in range(3 if z < 4 else 2)]

    copies = [pltpu.make_async_copy(a, b, done.at[i]) for i, (a, b) in enumerate(zip(near, outs))]
    for z in range(4):
        metal = fe[z, 2]
        for k in range(3):
            e = put_right(e1[z + 1, k], z, ends_e[k])[0:16]
            flow = HOLD * j1[k, z] - PULL * p1[k, z] + GAIN * metal * e
            j_near[k, z] = flow
            p_near[k, z] = p1[k, z] + time_step * flow
    copies[2].start()
    copies[3].start()
    e = fixed_e(-1)
    for z in range(-1, 4):
        up = fixed_e(z + 1)
        h = [h1[z + 1, 0]] + [put_right(h1[z + 1, k], z, ends_h[k]) for k in (1, 2)]
        x = after_x(e, z)
        new = magnetic_new(
            h,
            e,
            {0: y_next(e[0]), 2: y_next(e[2])},
            {0: up[0], 1: up[1]},
            {1: x(1), 2: x(2)},
            fh[z, 0] if z >= 0 else low[0],
            fh[z, 1] if z >= 0 else low[1],
        )
        for k in range(3):
            h2[z + 1, k] = new[k]
            if z >= 0:
                h_near[k, z] = new[k][0:16]
        e = up
    copies[1].start()
    for z in range(4):
        h = [h2[z + 1, k] for k in range(3)]
        down = [h2[z, k] for k in range(2)]
        x = before_x(h, z)
        new = electric_new(
            [a[0:16] for a in fixed_e(z)],
            [a[0:16] for a in h],
            {0: y_back(h[0])[0:16], 2: y_back(h[2])[0:16]},
            {0: down[0][0:16], 1: down[1][0:16]},
            {1: x(1)[0:16], 2: x(2)[0:16]},
            [fe[z, 2] * j_near[k, z] for k in range(3)],
            fe[z, 0],
            fe[z, 1],
        )
        for k in range(3):
            e_near[k, z] = new[k]
    copies[0].start()
    for copy in copies:
        copy.wait()


VMEM = pl.BlockSpec(memory_space=pltpu.VMEM)
HBM = pl.BlockSpec(memory_space=pltpu.HBM)


def call(kernel, outs, args, scratch=(), flops=0, size=0, far=False, far_out=False, name=None):
    size = size or sum(a.size for a in args) + sum(o.size for o in outs)
    return pl.pallas_call(
        kernel,
        out_shape=outs,
        in_specs=[HBM if far else VMEM] * len(args),
        out_specs=[HBM if far_out else VMEM] * len(outs),
        scratch_shapes=list(scratch),
        cost_estimate=pl.CostEstimate(flops=flops, bytes_accessed=4 * size, transcendentals=0),
        compiler_params=pltpu.CompilerParams(vmem_limit_bytes=16 * 2**20),
        name=name,
    )(*args)


def f32(*shape):
    return jax.ShapeDtypeStruct(shape, jnp.float32)


def on_device(electric, magnetic, polar, current, material, pml):
    cells = (electric, magnetic, polar, current, material, pml)
    gx, gy, gz = (lax.axis_size(a) for a in ("gx", "gy", "gz"))
    shapes = [jax.ShapeDtypeStruct(a.shape, a.dtype) for a in cells]
    cells = [pltpu.with_memory_space_constraint(a, pltpu.HBM) for a in cells]
    *cells, down = call(
        load_and_low_faces,
        [*shapes, f32(72, 128)],
        cells,
        scratch=[pltpu.SemaphoreType.DMA((6,))],
        far=True,
        name="load_and_low_faces",
    )
    ups, downs = up_of(gy), down_of(gy)
    after = lax.ppermute(down, "gy", [(i, j) for i, j in downs if i % 4 in (1, 2)])
    (up,) = call(high_faces, [f32(64, 128)], (*cells, down), size=HINT, name="high_faces")
    before = lax.ppermute(up, "gy", [(i, j) for i, j in ups if i % 4 != 2])
    down, mixed = call(last_faces, [f32(48, 128), f32(64, 128)], (down, up), size=HINT, name="last_faces")
    later = lax.ppermute(down, "gy", [(i, j) for i, j in downs if i % 4 == 0])
    last = lax.ppermute(mixed, "gy", [(i, j) for i, j in ups if i % 4 == 2] + [(i, j) for i, j in downs if i % 4 == 3])
    after, before = call(
        joined,
        [f32(48, 128), f32(64, 128)],
        (after, later, before),
        size=1 << 30,
        flops=1 << 36,
        name="joined",
    )
    wide, own = call(
        widen_rows,
        [f32(4, 10, ROWS, 128), f32(3, ROWS, 128)],
        (*cells, before, after, last),
        name="widen_rows",
    )
    pairs = [(i, i ^ 1) for i in range(gx) if i ^ 1 < gx]
    between = [(i, j) for i in range(1, gx - 1, 2) if i + 1 < gx for i, j in ((i, i + 1), (i + 1, i))]
    outer = lax.ppermute(own, "gx", pairs)
    inner = lax.ppermute(own, "gx", between)

    ring_up = [(i, (i + 1) % gz) for i in range(gz)]
    ring_down = [((i + 1) % gz, i) for i in range(gz)]
    brick, plane = f32(3, 4, 16, 128), (ROWS, 128)
    up, down, h1, r1, p1, j1, fh, fe, push = call(
        z_faces,
        [f32(Z_UP, *plane), f32(Z_DOWN, *plane), f32(4, 3, *plane), f32(4, 3, *plane), brick, brick]
        + [f32(4, 2, *plane), f32(4, 3, 16, 128), f32(4, *plane)],
        (wide, cells[2], own),
        flops=1_000_000,
        name="z_faces",
    )
    before = lax.ppermute(up, "gz", ring_up)
    after = lax.ppermute(down, "gz", ring_down)
    up, down = call(columns_on, [f32(72, 128), f32(73, 128)], (own, outer, inner), size=1 << 30, flops=1 << 36, name="columns_on")
    columns_before = lax.ppermute(up, "gz", ring_up)
    columns_after = lax.ppermute(down, "gz", ring_down)

    h1, e1, low = call(
        first_step,
        [f32(5, 3, *plane), f32(6, 3, *plane), f32(2, *plane)],
        (wide, before, after, h1, r1, fh, push),
        flops=1_000_000,
        name="first_step",
    )
    return tuple(
        call(
            second_step,
            [brick] * 4,
            (own, outer, inner, columns_before, columns_after, h1, e1, low, p1, j1, fh, fe),
            scratch=[pltpu.VMEM((3, 4, 16, 128), jnp.float32)] * 4
            + [pltpu.VMEM((5, 3, ROWS, 128), jnp.float32), pltpu.SemaphoreType.DMA((4,))],
            far_out=True,
            flops=2_000_000,
            name="second_step",
        )
    )


def solution(mesh):
    fields = P(None, "gz", "gy", "gx")
    cells = P("gz", "gy", "gx")
    return jax.shard_map(
        on_device,
        mesh=mesh,
        in_specs=(fields, fields, fields, fields, cells, cells),
        out_specs=(fields, fields, fields, fields),
        check_vma=False,
    )
```

```python
import jax
import jax.numpy as jnp
from jax import lax
from jax.experimental import pallas as pl
from jax.experimental.pallas import tpu as pltpu
from jax.sharding import PartitionSpec as P

time_step = 0.5
damping = 0.2
omega_sq = 1.0
strength = 3.0

DECAY = 1.0 + 0.5 * damping * time_step
HOLD = (1.0 - 0.5 * damping * time_step) / DECAY
PULL = time_step * omega_sq / DECAY
GAIN = PULL * strength

EX, EY, EZ, HX, HY, HZ, QX, QY, QZ, CODE = range(10)
EVERY = tuple(range(10))

Y_UP = [(c, 14) for c in (EX, EY, EZ, HX, HZ, CODE)] + [(c, 15) for c in EVERY]
Y_DOWN = [(c, 0) for c in (EX, EY, EZ, HX, HY, HZ, QX, QZ, CODE)] + [(EX, 1), (EZ, 1)]
Z_UP, Z_DOWN = 9, 8

ROWS = 24
SPAN = 32


def up_of(n):
    return [(i, i + 1) for i in range(n - 1)]


def down_of(n):
    return [(i + 1, i) for i in range(n - 1)]


def code_of(material, pml):
    return (1 + 4 * material + pml).astype(jnp.float32)


def y_face(cells, c, row):
    e, h, p, j, material, pml = cells
    if c < HX:
        return e[c, :, row, :]
    if c < QX:
        return h[c - HX, :, row, :]
    if c < CODE:
        return HOLD * j[c - QX, :, row, :] - PULL * p[c - QX, :, row, :]
    return code_of(material[:, row, :], pml[:, row, :])


def block_class():
    return lax.axis_index("gy") % 4


def load_and_faces(*refs):
    far, near, (down, up, late, mixed), done = refs[:6], refs[6:12], refs[12:16], refs[16]
    copies = [pltpu.make_async_copy(a, b, done.at[i]) for i, (a, b) in enumerate(zip(far, near))]
    for copy in copies:
        copy.start()
    for copy in copies:
        copy.wait()
    is_up = block_class() == 2
    down[...] = jnp.zeros_like(down)
    late[...] = jnp.zeros_like(late)
    for i, (c, row) in enumerate(Y_UP):
        value = y_face(near, c, row)
        at = slice(4 * i, 4 * i + 4)
        up[at, :] = value
        if i < len(Y_DOWN):
            low = y_face(near, *Y_DOWN[i])
            down[at, :] = low
            late[at, :] = low
            value = jnp.where(is_up, value, low)
        mixed[at, :] = value


def joined(after, later, before, rows_after, rows_before):
    rows_after[...] = after[0:48, :] + later[...]
    rows_before[...] = before[...]


def own_value(cells, c, z):
    e, h, p, j, material, pml = cells
    if c < HX:
        return e[c, z]
    if c < QX:
        return h[c - HX, z]
    if c < CODE:
        return HOLD * j[c - QX, z] - PULL * p[c - QX, z]
    return code_of(material[z], pml[z])


def edge_columns(value, g, rows):
    lane = lax.broadcasted_iota(jnp.int32, (rows, 128), 1)
    total = jnp.zeros((rows, 128), jnp.float32)
    for c in range(4 * g, min(4 * g + 4, 10)):
        for z in range(4):
            at = SPAN * (c - 4 * g) + 4 * (z + 2)
            total = jnp.where((lane >= at) & (lane < at + 4), roll(value(c, z), at - 126, 1), total)
    return total


def own_planes(*refs):
    cells, (planes, edges, p1, j1, fe) = refs[:6], refs[6:]
    for z in range(4):
        _, _, keep_e, push_e, metal = factors(own_value(cells, CODE, z))
        for k, f in enumerate((keep_e, push_e, metal)):
            fe[z, k] = f
        for k in range(3):
            flow = own_value(cells, QX + k, z) + GAIN * metal * cells[0][k, z]
            j1[k, z] = flow
            p1[k, z] = cells[2][k, z] + time_step * flow
        for c in EVERY:
            planes[z, c] = own_value(cells, c, z)
    for g in range(3):
        edges[g] = edge_columns(lambda c, z: own_value(cells, c, z), g, 16)


def widen_rows(before, after, last, own, beside, edges):
    low, high = block_class() == 3, block_class() == 2
    beside[...] = jnp.zeros_like(beside)
    for z in range(4):
        for i, (c, row) in enumerate(Y_UP):
            at = slice(4 * i + z, 4 * i + z + 1)
            beside[z, c, row - 8 : row - 7, :] = jnp.where(low, last[at, :], before[at, :])
        for i, (c, row) in enumerate(Y_DOWN):
            at = slice(4 * i + z, 4 * i + z + 1)
            beside[z, c, row : row + 1, :] = jnp.where(high, last[at, :], after[at, :])
    for g in range(3):
        edges[g, 0:16, :] = own[g]
        edges[g, 16:24, :] = edge_columns(lambda c, z: beside[z, c], g, 8)


def widened(planes, beside, z, c):
    return jnp.concatenate([planes[z, c], beside[z, c]])


def z_faces(planes, beside, _, up, down, h1, r1, fh, push):
    wide = [[widened(planes, beside, z, c) for c in EVERY] for z in range(4)]
    for z in range(4):
        e = wide[z][EX : EZ + 1]
        h = wide[z][HX : HZ + 1]
        keep_h, push_h, keep_e, push_e, metal = factors(wide[z][CODE])
        later = [wide[z + 1][EX + k] for k in range(2)] if z < 3 else [0.0, 0.0]
        new = magnetic_new(
            h,
            e,
            {0: y_next(e[0]), 2: y_next(e[2])},
            {0: later[0], 1: later[1]},
            {1: x_next(e[1]), 2: x_next(e[2])},
            keep_h,
            push_h,
        )
        flow = [wide[z][QX + k] + GAIN * metal * e[k] for k in range(3)]
        rest = [keep_e * e[k] - push_e * (metal * flow[k]) for k in range(3)]
        for k in range(3):
            h1[z, k] = new[k]
            r1[z, k] = rest[k]
        fh[z, 0] = keep_h
        fh[z, 1] = push_h
        push[z] = push_e
        if z == 0:
            for i, value in enumerate(new + rest[:2] + [wide[z][CODE]] + e[:2]):
                down[i] = value
        if z == 2:
            up[7] = new[0]
            up[8] = new[1]
        if z == 3:
            for i, value in enumerate(new + rest + [wide[z][CODE]]):
                up[i] = value


def sides(own, outer, inner, g):
    near = (lanes() % 4) < 2
    odd = lax.axis_index("gx") % 2 == 1
    left = jnp.where(odd, outer[g], inner[g])
    right = jnp.where(odd, inner[g], outer[g])
    return jnp.where(near, left, own[g]), jnp.where(near, own[g], right)


def columns_on(own, outer, inner, *outs):
    part = (lanes() % SPAN) // 8
    for g in range(3):
        low, high = sides(own, outer, inner, g)
        up = jnp.where(part == 0, roll(low, -16, 1), roll(high, -8, 1))
        down = jnp.where(part == 2, roll(high, 8, 1), roll(low, 16, 1))
        for out in outs:
            out[ROWS * g : ROWS * (g + 1), :] = jnp.where(part < 2, up, down)


def grid_ends():
    place = lax.axis_index("gz")
    return place == 0, place == lax.axis_size("gz") - 1


def lanes():
    return lax.broadcasted_iota(jnp.int32, (ROWS, 128), 1)


def roll(array, shift, axis):
    shift = shift % array.shape[axis]
    return pltpu.roll(array, shift, axis) if shift else array


def factors(code):
    metal = code > 8.5
    dielec = (code > 4.5) & (code < 8.5)
    inside = code > 0.5
    level = code - jnp.where(metal, 9.0, jnp.where(dielec, 5.0, 1.0))
    loss = jnp.where(level > 2.5, 0.25, jnp.where(level > 1.5, 0.1, jnp.where(level > 0.5, 0.025, 0.0)))
    permit = jnp.where(metal, 1.5, jnp.where(dielec, 2.25, 1.0))
    over_h = jnp.where(inside, 1.0 / (1.0 + loss), 0.0)
    over_e = jnp.where(inside, 1.0 / (permit + loss), 0.0)
    return (
        (1.0 - loss) * over_h,
        time_step * over_h,
        (permit - loss) * over_e,
        time_step * over_e,
        jnp.where(metal, 1.0, 0.0),
    )


def magnetic_new(h, e, ey, ez, ex, keep, push):
    curl = (
        (ey[2] - e[2]) - (ez[1] - e[1]),
        (ez[0] - e[0]) - (ex[2] - e[2]),
        (ex[1] - e[1]) - (ey[0] - e[0]),
    )
    return [None if h[k] is None else keep * h[k] - push * curl[k] for k in range(3)]


def curl_back(h, hy, hz, hx):
    return (
        (h[2] - hy[2]) - (h[1] - hz[1]),
        (h[0] - hz[0]) - (h[2] - hx[2]),
        (h[1] - hx[1]) - (h[0] - hy[0]),
    )


def electric_new(e, h, hy, hz, hx, drag, keep, push):
    curl = curl_back(h, hy, hz, hx)
    return [keep * e[k] + push * (curl[k] - drag[k]) for k in range(3)]


x_next = lambda a: roll(a, -1, 1)
x_back = lambda a: roll(a, 1, 1)
y_next = lambda a: roll(a, -1, 0)
y_back = lambda a: roll(a, 1, 0)


def first_step(planes, beside, before, after, part, r1, fh, push, h1, e1, low):
    first, last = grid_ends()

    def from_below(i):
        return jnp.where(first, 0.0, before[i])

    def from_above(i):
        return jnp.where(last, 0.0, after[i])

    def with_next(h, push_h, x, y):
        return [h[0] + push_h * y, h[1] - push_h * x, h[2]]

    def electric(z, rest, push_e, h, back):
        curl = curl_back(
            h,
            {0: y_back(h[0]), 2: y_back(h[2])},
            {0: back[0], 1: back[1]},
            {1: x_back(h[1]), 2: x_back(h[2])},
        )
        for k, r in enumerate(rest):
            e1[z + 1, k] = r + push_e * curl[k]

    keep_h, push_h, _, push_e, _ = factors(from_below(6))
    low[0] = keep_h
    low[1] = push_h
    h = with_next([from_below(k) for k in range(3)], push_h, widened(planes, beside, 0, EX), widened(planes, beside, 0, EY))
    electric(-1, [from_below(3 + k) for k in range(3)], push_e, h, [from_below(7), from_below(8)])
    for z in range(4):
        for k in range(3):
            h1[z, k] = h[k]
        back, h = h, [part[z, k] for k in range(3)]
        if z == 3:
            h = with_next(h, fh[z, 1], from_above(6), from_above(7))
        electric(z, [r1[z, k] for k in range(3)], push[z], h, back)
    for k in range(3):
        h1[4, k] = h[k]
    _, _, _, push_e, _ = factors(from_above(5))
    electric(4, [from_above(3 + k) for k in range(2)], push_e, [from_above(k) for k in range(3)], h)


def columns(own, outer, inner, before, after):
    first, last = grid_ends()
    lane = lanes()
    part = (lane % SPAN) // 8
    values = []
    for g in range(3):
        low, high = sides(own, outer, inner, g)
        rows = slice(ROWS * g, ROWS * (g + 1))
        up = jnp.where(first, 0.0, before[rows, :])
        down = jnp.where(last, 0.0, after[rows, :])
        low = jnp.where(part == 0, up, jnp.where(part == 3, down, low))
        high = jnp.where(part == 0, roll(up, -8, 1), jnp.where(part == 3, roll(down, 8, 1), high))
        for k in range(4):
            values.append(jnp.where(lane < SPAN, roll(low, -SPAN * k, 1), roll(high, SPAN - SPAN * k, 1)))
    z_next = lambda a: roll(a, -4, 1)
    z_back = lambda a: roll(a, 4, 1)

    def shifted(f, y, z, x):
        return {0: y(f[0]), 2: y(f[2])}, {0: z(f[0]), 1: z(f[1])}, {1: x(f[1]), 2: x(f[2])}

    keep_h, push_h, keep_e, push_e, metal = factors(values[CODE])
    e0 = values[EX : EZ + 1]
    h1 = magnetic_new(values[HX : HZ + 1], e0, *shifted(e0, y_next, z_next, x_next), keep_h, push_h)
    drag = [metal * (values[QX + k] + GAIN * e0[k]) for k in range(3)]
    e1 = electric_new(e0, h1, *shifted(h1, y_back, z_back, x_back), drag, keep_e, push_e)
    h2 = magnetic_new(h1, e1, *shifted(e1, y_next, z_next, x_next), keep_h, push_h)
    return h1, e1, h2


def second_step(own, outer, inner, before, after, h1, e1, low, p1, j1, fh, fe, *rest):
    outs, near, h2, fixed, done = rest[:4], rest[4:8], rest[8], rest[9], rest[10]
    e_near, h_near, p_near, j_near = near
    lane = lanes()
    ch1, ce1, ch2 = columns(own, outer, inner, before, after)

    def at_ends(column):
        return jnp.where(lane % 4 == 1, roll(column, -SPAN, 1), column)

    def put_right(array, z, column):
        return jnp.where((lane == 0) | (lane == 127), roll(column, 127 - (4 * (z + 2) + 1), 1), array)

    ends_h = [at_ends(a) for a in ch1]
    ends_e = [at_ends(a) for a in ce1]

    def after_x(array, z):
        return lambda k: jnp.where(lane == 127, roll(ce1[k], 127 - (SPAN + 4 * (z + 2) + 2), 1), x_next(array[k]))

    def before_x(array, z):
        return lambda k: jnp.where(lane == 0, roll(ch2[k], -(4 * (z + 2) + 1), 1), x_back(array[k]))

    def fixed_e(z):
        return [put_right(e1[z + 1, k], z, ends_e[k]) for k in range(3 if z < 4 else 2)]

    for z in range(-1, 5):
        for k, a in enumerate(fixed_e(z)):
            fixed[z + 1, k] = a
    copies = [pltpu.make_async_copy(a, b, done.at[i]) for i, (a, b) in enumerate(zip(near, outs))]
    for z in range(4):
        metal = fe[z, 2]
        for k in range(3):
            e = fixed[z + 1, k, 0:16, :]
            flow = HOLD * j1[k, z] - PULL * p1[k, z] + GAIN * metal * e
            j_near[k, z] = flow
            p_near[k, z] = p1[k, z] + time_step * flow
    copies[2].start()
    copies[3].start()
    e = [fixed[0, k] for k in range(3)]
    for z in range(-1, 4):
        up = [fixed[z + 2, k] for k in range(3 if z < 3 else 2)]
        h = [h1[z + 1, 0]] + [put_right(h1[z + 1, k], z, ends_h[k]) for k in (1, 2)]
        x = after_x(e, z)
        new = magnetic_new(
            h,
            e,
            {0: y_next(e[0]), 2: y_next(e[2])},
            {0: up[0], 1: up[1]},
            {1: x(1), 2: x(2)},
            fh[z, 0] if z >= 0 else low[0],
            fh[z, 1] if z >= 0 else low[1],
        )
        for k in range(3):
            h2[z + 1, k] = new[k]
            if z >= 0:
                h_near[k, z] = new[k][0:16]
        e = up
    copies[1].start()
    for z in range(4):
        h = [h2[z + 1, k] for k in range(3)]
        down = [h2[z, k] for k in range(2)]
        x = before_x(h, z)
        new = electric_new(
            [fixed[z + 1, k, 0:16, :] for k in range(3)],
            [a[0:16] for a in h],
            {0: y_back(h[0])[0:16], 2: y_back(h[2])[0:16]},
            {0: down[0][0:16], 1: down[1][0:16]},
            {1: x(1)[0:16], 2: x(2)[0:16]},
            [fe[z, 2] * j_near[k, z] for k in range(3)],
            fe[z, 0],
            fe[z, 1],
        )
        for k in range(3):
            e_near[k, z] = new[k]
    copies[0].start()
    for copy in copies:
        copy.wait()


VMEM = pl.BlockSpec(memory_space=pltpu.VMEM)
HBM = pl.BlockSpec(memory_space=pltpu.HBM)


def call(kernel, outs, args, scratch=(), flops=0, size=0, far=False, far_out=False, name=None):
    size = size or sum(a.size for a in args) + sum(o.size for o in outs)
    return pl.pallas_call(
        kernel,
        out_shape=outs,
        in_specs=[HBM if far else VMEM] * len(args),
        out_specs=[HBM if far_out else VMEM] * len(outs),
        scratch_shapes=list(scratch),
        cost_estimate=pl.CostEstimate(flops=flops, bytes_accessed=4 * size, transcendentals=0),
        compiler_params=pltpu.CompilerParams(vmem_limit_bytes=16 * 2**20),
        name=name,
    )(*args)


def f32(*shape):
    return jax.ShapeDtypeStruct(shape, jnp.float32)


def on_device(electric, magnetic, polar, current, material, pml):
    cells = (electric, magnetic, polar, current, material, pml)
    gx, gy, gz = (lax.axis_size(a) for a in ("gx", "gy", "gz"))
    shapes = [jax.ShapeDtypeStruct(a.shape, a.dtype) for a in cells]
    cells = [pltpu.with_memory_space_constraint(a, pltpu.HBM) for a in cells]
    *cells, down, up, late, mixed = call(
        load_and_faces,
        [*shapes, f32(72, 128), f32(64, 128), f32(48, 128), f32(64, 128)],
        cells,
        scratch=[pltpu.SemaphoreType.DMA((6,))],
        far=True,
        name="load_and_faces",
    )
    ups, downs = up_of(gy), down_of(gy)
    after = lax.ppermute(down, "gy", [(i, j) for i, j in downs if i % 4 in (1, 2)])
    before = lax.ppermute(up, "gy", [(i, j) for i, j in ups if i % 4 != 2])
    later = lax.ppermute(late, "gy", [(i, j) for i, j in downs if i % 4 == 0])
    last = lax.ppermute(mixed, "gy", [(i, j) for i, j in ups if i % 4 == 2] + [(i, j) for i, j in downs if i % 4 == 3])
    after, before = call(
        joined,
        [f32(48, 128), f32(64, 128)],
        (after, later, before),
        size=1 << 30,
        flops=1 << 36,
        name="joined",
    )
    brick, plane = f32(3, 4, 16, 128), (ROWS, 128)
    planes, own, p1, j1, fe = call(
        own_planes,
        [f32(4, 10, 16, 128), f32(3, 16, 128), brick, brick, f32(4, 3, 16, 128)],
        cells,
        name="own_planes",
    )
    beside, own = call(
        widen_rows,
        [f32(4, 10, 8, 128), f32(3, *plane)],
        (before, after, last, own),
        name="widen_rows",
    )
    pairs = [(i, i ^ 1) for i in range(gx) if i ^ 1 < gx]
    between = [(i, j) for i in range(1, gx - 1, 2) if i + 1 < gx for i, j in ((i, i + 1), (i + 1, i))]
    outer = lax.ppermute(own, "gx", pairs)
    inner = lax.ppermute(own, "gx", between)

    ring_up = [(i, (i + 1) % gz) for i in range(gz)]
    ring_down = [((i + 1) % gz, i) for i in range(gz)]
    up, down, h1, r1, fh, push = call(
        z_faces,
        [f32(Z_UP, *plane), f32(Z_DOWN, *plane), f32(4, 3, *plane), f32(4, 3, *plane)]
        + [f32(4, 2, *plane), f32(4, *plane)],
        (planes, beside, own),
        flops=1_000_000,
        name="z_faces",
    )
    before = lax.ppermute(up, "gz", ring_up)
    after = lax.ppermute(down, "gz", ring_down)
    up, down = call(columns_on, [f32(72, 128), f32(73, 128)], (own, outer, inner), size=1 << 30, flops=1 << 36, name="columns_on")
    columns_before = lax.ppermute(up, "gz", ring_up)
    columns_after = lax.ppermute(down, "gz", ring_down)

    h1, e1, low = call(
        first_step,
        [f32(5, 3, *plane), f32(6, 3, *plane), f32(2, *plane)],
        (planes, beside, before, after, h1, r1, fh, push),
        flops=1_000_000,
        name="first_step",
    )
    return tuple(
        call(
            second_step,
            [brick] * 4,
            (own, outer, inner, columns_before, columns_after, h1, e1, low, p1, j1, fh, fe),
            scratch=[pltpu.VMEM((3, 4, 16, 128), jnp.float32)] * 4
            + [pltpu.VMEM((5, 3, ROWS, 128), jnp.float32), pltpu.VMEM((6, 3, ROWS, 128), jnp.float32), pltpu.SemaphoreType.DMA((4,))],
            far_out=True,
            flops=2_000_000,
            name="second_step",
        )
    )


def solution(mesh):
    fields = P(None, "gz", "gy", "gx")
    cells = P("gz", "gy", "gx")
    return jax.shard_map(
        on_device,
        mesh=mesh,
        in_specs=(fields, fields, fields, fields, cells, cells),
        out_specs=(fields, fields, fields, fields),
        check_vma=False,
    )
```

```python
import jax
import jax.numpy as jnp
from jax import lax
from jax.experimental import pallas as pl
from jax.experimental.pallas import tpu as pltpu
from jax.sharding import PartitionSpec as P

time_step = 0.5
damping = 0.2
omega_sq = 1.0
strength = 3.0

DECAY = 1.0 + 0.5 * damping * time_step
HOLD = (1.0 - 0.5 * damping * time_step) / DECAY
PULL = time_step * omega_sq / DECAY
GAIN = PULL * strength

EX, EY, EZ, HX, HY, HZ, QX, QY, QZ, CODE = range(10)
EVERY = tuple(range(10))

Y_UP = [(c, 14) for c in (EX, EY, EZ, HX, HZ, CODE)] + [(c, 15) for c in EVERY]
Y_DOWN = [(c, 0) for c in (EX, EY, EZ, HX, HY, HZ, QX, QZ, CODE)] + [(EX, 1), (EZ, 1)]
Z_UP, Z_DOWN = 9, 8

ROWS = 24
SPAN = 32


def up_of(n):
    return [(i, i + 1) for i in range(n - 1)]


def down_of(n):
    return [(i + 1, i) for i in range(n - 1)]


def code_of(material, pml):
    return (1 + 4 * material + pml).astype(jnp.float32)


def y_face(cells, c, row):
    e, h, p, j, material, pml = cells
    if c < HX:
        return e[c, :, row, :]
    if c < QX:
        return h[c - HX, :, row, :]
    if c < CODE:
        return HOLD * j[c - QX, :, row, :] - PULL * p[c - QX, :, row, :]
    return code_of(material[:, row, :], pml[:, row, :])


def block_class():
    return lax.axis_index("gy") % 4


def load_and_faces(*refs):
    far, near, (down, up, late, mixed), done = refs[:6], refs[6:12], refs[12:16], refs[16]
    copies = [pltpu.make_async_copy(a, b, done.at[i]) for i, (a, b) in enumerate(zip(far, near))]
    for copy in copies:
        copy.start()
    for copy in copies:
        copy.wait()
    is_up = block_class() == 2
    down[...] = jnp.zeros_like(down)
    late[...] = jnp.zeros_like(late)
    for i, (c, row) in enumerate(Y_UP):
        value = y_face(near, c, row)
        at = slice(4 * i, 4 * i + 4)
        up[at, :] = value
        if i < len(Y_DOWN):
            low = y_face(near, *Y_DOWN[i])
            down[at, :] = low
            late[at, :] = low
            value = jnp.where(is_up, value, low)
        mixed[at, :] = value


def joined(after, later, before, rows_after, rows_before):
    rows_after[...] = after[0:48, :] + later[...]
    rows_before[...] = before[...]


def own_value(cells, c, z):
    e, h, p, j, material, pml = cells
    if c < HX:
        return e[c, z]
    if c < QX:
        return h[c - HX, z]
    if c < CODE:
        return HOLD * j[c - QX, z] - PULL * p[c - QX, z]
    return code_of(material[z], pml[z])


def edge_columns(value, g, rows):
    lane = lax.broadcasted_iota(jnp.int32, (rows, 128), 1)
    total = jnp.zeros((rows, 128), jnp.float32)
    starts = [(4 * g + k, SPAN * k) for k in range(4)]
    if g == 0:
        starts += [(8, SPAN // 2), (9, SPAN + SPAN // 2)]
    for c, start in starts:
        for z in range(4):
            at = start + 4 * (z + 2)
            total = jnp.where((lane >= at) & (lane < at + 4), roll(value(c, z), at - 126, 1), total)
    return total


def own_planes(*refs):
    cells, (planes, edges, p1, j1, fe) = refs[:6], refs[6:]
    for z in range(4):
        _, _, keep_e, push_e, metal = factors(own_value(cells, CODE, z))
        for k, f in enumerate((keep_e, push_e, metal)):
            fe[z, k] = f
        for k in range(3):
            flow = own_value(cells, QX + k, z) + GAIN * metal * cells[0][k, z]
            j1[k, z] = flow
            p1[k, z] = cells[2][k, z] + time_step * flow
        for c in EVERY:
            planes[z, c] = own_value(cells, c, z)
    for g in range(2):
        edges[g] = edge_columns(lambda c, z: own_value(cells, c, z), g, 16)


def widen_rows(before, after, last, own, beside, edges):
    low, high = block_class() == 3, block_class() == 2
    beside[...] = jnp.zeros_like(beside)
    for z in range(4):
        for i, (c, row) in enumerate(Y_UP):
            at = slice(4 * i + z, 4 * i + z + 1)
            beside[z, c, row - 8 : row - 7, :] = jnp.where(low, last[at, :], before[at, :])
        for i, (c, row) in enumerate(Y_DOWN):
            at = slice(4 * i + z, 4 * i + z + 1)
            beside[z, c, row : row + 1, :] = jnp.where(high, last[at, :], after[at, :])
    for g in range(2):
        edges[g, 0:16, :] = own[g]
        edges[g, 16:24, :] = edge_columns(lambda c, z: beside[z, c], g, 8)


def widened(planes, beside, z, c):
    return jnp.concatenate([planes[z, c], beside[z, c]])


def z_faces(planes, beside, _, up, down, h1, r1, fh, push):
    wide = [[widened(planes, beside, z, c) for c in EVERY] for z in range(4)]
    for z in range(4):
        e = wide[z][EX : EZ + 1]
        h = wide[z][HX : HZ + 1]
        keep_h, push_h, keep_e, push_e, metal = factors(wide[z][CODE])
        later = [wide[z + 1][EX + k] for k in range(2)] if z < 3 else [0.0, 0.0]
        new = magnetic_new(
            h,
            e,
            {0: y_next(e[0]), 2: y_next(e[2])},
            {0: later[0], 1: later[1]},
            {1: x_next(e[1]), 2: x_next(e[2])},
            keep_h,
            push_h,
        )
        flow = [wide[z][QX + k] + GAIN * metal * e[k] for k in range(3)]
        rest = [keep_e * e[k] - push_e * (metal * flow[k]) for k in range(3)]
        for k in range(3):
            h1[z, k] = new[k]
            r1[z, k] = rest[k]
        fh[z, 0] = keep_h
        fh[z, 1] = push_h
        push[z] = push_e
        if z == 0:
            for i, value in enumerate(new + rest[:2] + [wide[z][CODE]] + e[:2]):
                down[i] = value
        if z == 2:
            up[7] = new[0]
            up[8] = new[1]
        if z == 3:
            for i, value in enumerate(new + rest + [wide[z][CODE]]):
                up[i] = value


def sides(own, outer, inner, g):
    if g == 2:
        return [roll(a, -SPAN // 2, 1) for a in sides(own, outer, inner, 0)]
    near = (lanes() % 4) < 2
    odd = lax.axis_index("gx") % 2 == 1
    left = jnp.where(odd, outer[g], inner[g])
    right = jnp.where(odd, inner[g], outer[g])
    return jnp.where(near, left, own[g]), jnp.where(near, own[g], right)


def columns_on(own, outer, inner, lows, highs, *outs):
    part = (lanes() % SPAN) // 8
    for g in range(3):
        low, high = sides(own, outer, inner, g)
        lows[g], highs[g] = low, high
        up = jnp.where(part == 0, roll(low, -16, 1), roll(high, -8, 1))
        down = jnp.where(part == 2, roll(high, 8, 1), roll(low, 16, 1))
        for out in outs:
            out[ROWS * g : ROWS * (g + 1), :] = jnp.where(part < 2, up, down)


def grid_ends():
    place = lax.axis_index("gz")
    return place == 0, place == lax.axis_size("gz") - 1


def lanes():
    return lax.broadcasted_iota(jnp.int32, (ROWS, 128), 1)


def roll(array, shift, axis):
    shift = shift % array.shape[axis]
    return pltpu.roll(array, shift, axis) if shift else array


def factors(code):
    metal = code > 8.5
    dielec = (code > 4.5) & (code < 8.5)
    inside = code > 0.5
    level = code - jnp.where(metal, 9.0, jnp.where(dielec, 5.0, 1.0))
    loss = jnp.where(level > 2.5, 0.25, jnp.where(level > 1.5, 0.1, jnp.where(level > 0.5, 0.025, 0.0)))
    permit = jnp.where(metal, 1.5, jnp.where(dielec, 2.25, 1.0))
    over_h = jnp.where(inside, 1.0 / (1.0 + loss), 0.0)
    over_e = jnp.where(inside, 1.0 / (permit + loss), 0.0)
    return (
        (1.0 - loss) * over_h,
        time_step * over_h,
        (permit - loss) * over_e,
        time_step * over_e,
        jnp.where(metal, 1.0, 0.0),
    )


def magnetic_new(h, e, ey, ez, ex, keep, push):
    curl = (
        (ey[2] - e[2]) - (ez[1] - e[1]),
        (ez[0] - e[0]) - (ex[2] - e[2]),
        (ex[1] - e[1]) - (ey[0] - e[0]),
    )
    return [None if h[k] is None else keep * h[k] - push * curl[k] for k in range(3)]


def curl_back(h, hy, hz, hx):
    return (
        (h[2] - hy[2]) - (h[1] - hz[1]),
        (h[0] - hz[0]) - (h[2] - hx[2]),
        (h[1] - hx[1]) - (h[0] - hy[0]),
    )


def electric_new(e, h, hy, hz, hx, drag, keep, push):
    curl = curl_back(h, hy, hz, hx)
    return [keep * e[k] + push * (curl[k] - drag[k]) for k in range(3)]


x_next = lambda a: roll(a, -1, 1)
x_back = lambda a: roll(a, 1, 1)
y_next = lambda a: roll(a, -1, 0)
y_back = lambda a: roll(a, 1, 0)


def first_step(planes, beside, before, after, part, r1, fh, push, h1, e1, low):
    first, last = grid_ends()

    def from_below(i):
        return jnp.where(first, 0.0, before[i])

    def from_above(i):
        return jnp.where(last, 0.0, after[i])

    def with_next(h, push_h, x, y):
        return [h[0] + push_h * y, h[1] - push_h * x, h[2]]

    def electric(z, rest, push_e, h, back):
        curl = curl_back(
            h,
            {0: y_back(h[0]), 2: y_back(h[2])},
            {0: back[0], 1: back[1]},
            {1: x_back(h[1]), 2: x_back(h[2])},
        )
        for k, r in enumerate(rest):
            e1[z + 1, k] = r + push_e * curl[k]

    keep_h, push_h, _, push_e, _ = factors(from_below(6))
    low[0] = keep_h
    low[1] = push_h
    h = with_next([from_below(k) for k in range(3)], push_h, widened(planes, beside, 0, EX), widened(planes, beside, 0, EY))
    electric(-1, [from_below(3 + k) for k in range(3)], push_e, h, [from_below(7), from_below(8)])
    for z in range(4):
        for k in range(3):
            h1[z, k] = h[k]
        back, h = h, [part[z, k] for k in range(3)]
        if z == 3:
            h = with_next(h, fh[z, 1], from_above(6), from_above(7))
        electric(z, [r1[z, k] for k in range(3)], push[z], h, back)
    for k in range(3):
        h1[4, k] = h[k]
    _, _, _, push_e, _ = factors(from_above(5))
    electric(4, [from_above(3 + k) for k in range(2)], push_e, [from_above(k) for k in range(3)], h)


def columns(lows, highs, before, after):
    first, last = grid_ends()
    lane = lanes()
    part = (lane % SPAN) // 8
    values = []
    for g in range(3):
        low, high = lows[g], highs[g]
        rows = slice(ROWS * g, ROWS * (g + 1))
        up = jnp.where(first, 0.0, before[rows, :])
        down = jnp.where(last, 0.0, after[rows, :])
        low = jnp.where(part == 0, up, jnp.where(part == 3, down, low))
        high = jnp.where(part == 0, roll(up, -8, 1), jnp.where(part == 3, roll(down, 8, 1), high))
        for k in range(4):
            values.append(jnp.where(lane < SPAN, roll(low, -SPAN * k, 1), roll(high, SPAN - SPAN * k, 1)))
    z_next = lambda a: roll(a, -4, 1)
    z_back = lambda a: roll(a, 4, 1)

    def shifted(f, y, z, x):
        return {0: y(f[0]), 2: y(f[2])}, {0: z(f[0]), 1: z(f[1])}, {1: x(f[1]), 2: x(f[2])}

    keep_h, push_h, keep_e, push_e, metal = factors(values[CODE])
    e0 = values[EX : EZ + 1]
    h1 = magnetic_new(values[HX : HZ + 1], e0, *shifted(e0, y_next, z_next, x_next), keep_h, push_h)
    drag = [metal * (values[QX + k] + GAIN * e0[k]) for k in range(3)]
    e1 = electric_new(e0, h1, *shifted(h1, y_back, z_back, x_back), drag, keep_e, push_e)
    h2 = magnetic_new(h1, e1, *shifted(e1, y_next, z_next, x_next), keep_h, push_h)
    return h1, e1, h2


def second_step(lows, highs, before, after, h1, e1, low, p1, j1, fh, fe, *rest):
    outs, near, h2, fixed, done = rest[:4], rest[4:8], rest[8], rest[9], rest[10]
    e_near, h_near, p_near, j_near = near
    lane = lanes()
    ch1, ce1, ch2 = columns(lows, highs, before, after)

    def at_ends(column):
        return jnp.where(lane % 4 == 1, roll(column, -SPAN, 1), column)

    def put_right(array, z, column):
        return jnp.where((lane == 0) | (lane == 127), roll(column, 127 - (4 * (z + 2) + 1), 1), array)

    ends_h = [at_ends(a) for a in ch1]
    ends_e = [at_ends(a) for a in ce1]

    def after_x(array, z):
        return lambda k: jnp.where(lane == 127, roll(ce1[k], 127 - (SPAN + 4 * (z + 2) + 2), 1), x_next(array[k]))

    def before_x(array, z):
        return lambda k: jnp.where(lane == 0, roll(ch2[k], -(4 * (z + 2) + 1), 1), x_back(array[k]))

    def fixed_e(z):
        return [put_right(e1[z + 1, k], z, ends_e[k]) for k in range(3 if z < 4 else 2)]

    for z in range(-1, 5):
        for k, a in enumerate(fixed_e(z)):
            fixed[z + 1, k] = a
    copies = [pltpu.make_async_copy(a, b, done.at[i]) for i, (a, b) in enumerate(zip(near, outs))]
    for z in range(4):
        metal = fe[z, 2]
        for k in range(3):
            e = fixed[z + 1, k, 0:16, :]
            flow = HOLD * j1[k, z] - PULL * p1[k, z] + GAIN * metal * e
            j_near[k, z] = flow
            p_near[k, z] = p1[k, z] + time_step * flow
    copies[2].start()
    copies[3].start()
    e = [fixed[0, k] for k in range(3)]
    for z in range(-1, 4):
        up = [fixed[z + 2, k] for k in range(3 if z < 3 else 2)]
        h = [h1[z + 1, 0]] + [put_right(h1[z + 1, k], z, ends_h[k]) for k in (1, 2)]
        x = after_x(e, z)
        new = magnetic_new(
            h,
            e,
            {0: y_next(e[0]), 2: y_next(e[2])},
            {0: up[0], 1: up[1]},
            {1: x(1), 2: x(2)},
            fh[z, 0] if z >= 0 else low[0],
            fh[z, 1] if z >= 0 else low[1],
        )
        for k in range(3):
            h2[z + 1, k] = new[k]
            if z >= 0:
                h_near[k, z] = new[k][0:16]
        e = up
    copies[1].start()
    for z in range(4):
        h = [h2[z + 1, k] for k in range(3)]
        down = [h2[z, k] for k in range(2)]
        x = before_x(h, z)
        new = electric_new(
            [fixed[z + 1, k, 0:16, :] for k in range(3)],
            [a[0:16] for a in h],
            {0: y_back(h[0])[0:16], 2: y_back(h[2])[0:16]},
            {0: down[0][0:16], 1: down[1][0:16]},
            {1: x(1)[0:16], 2: x(2)[0:16]},
            [fe[z, 2] * j_near[k, z] for k in range(3)],
            fe[z, 0],
            fe[z, 1],
        )
        for k in range(3):
            e_near[k, z] = new[k]
    copies[0].start()
    for copy in copies:
        copy.wait()


VMEM = pl.BlockSpec(memory_space=pltpu.VMEM)
HBM = pl.BlockSpec(memory_space=pltpu.HBM)


def call(kernel, outs, args, scratch=(), flops=0, size=0, far=False, far_out=False, name=None):
    size = size or sum(a.size for a in args) + sum(o.size for o in outs)
    return pl.pallas_call(
        kernel,
        out_shape=outs,
        in_specs=[HBM if far else VMEM] * len(args),
        out_specs=[HBM if far_out else VMEM] * len(outs),
        scratch_shapes=list(scratch),
        cost_estimate=pl.CostEstimate(flops=flops, bytes_accessed=4 * size, transcendentals=0),
        compiler_params=pltpu.CompilerParams(vmem_limit_bytes=16 * 2**20),
        name=name,
    )(*args)


def f32(*shape):
    return jax.ShapeDtypeStruct(shape, jnp.float32)


def on_device(electric, magnetic, polar, current, material, pml):
    cells = (electric, magnetic, polar, current, material, pml)
    gx, gy, gz = (lax.axis_size(a) for a in ("gx", "gy", "gz"))
    shapes = [jax.ShapeDtypeStruct(a.shape, a.dtype) for a in cells]
    cells = [pltpu.with_memory_space_constraint(a, pltpu.HBM) for a in cells]
    *cells, down, up, late, mixed = call(
        load_and_faces,
        [*shapes, f32(72, 128), f32(64, 128), f32(48, 128), f32(64, 128)],
        cells,
        scratch=[pltpu.SemaphoreType.DMA((6,))],
        far=True,
        name="load_and_faces",
    )
    ups, downs = up_of(gy), down_of(gy)
    after = lax.ppermute(down, "gy", [(i, j) for i, j in downs if i % 4 in (1, 2)])
    before = lax.ppermute(up, "gy", [(i, j) for i, j in ups if i % 4 != 2])
    later = lax.ppermute(late, "gy", [(i, j) for i, j in downs if i % 4 == 0])
    last = lax.ppermute(mixed, "gy", [(i, j) for i, j in ups if i % 4 == 2] + [(i, j) for i, j in downs if i % 4 == 3])
    after, before = call(
        joined,
        [f32(48, 128), f32(64, 128)],
        (after, later, before),
        size=1 << 30,
        flops=1 << 36,
        name="joined",
    )
    brick, plane = f32(3, 4, 16, 128), (ROWS, 128)
    planes, own, p1, j1, fe = call(
        own_planes,
        [f32(4, 10, 16, 128), f32(2, 16, 128), brick, brick, f32(4, 3, 16, 128)],
        cells,
        name="own_planes",
    )
    beside, own = call(
        widen_rows,
        [f32(4, 10, 8, 128), f32(2, *plane)],
        (before, after, last, own),
        name="widen_rows",
    )
    pairs = [(i, i ^ 1) for i in range(gx) if i ^ 1 < gx]
    between = [(i, j) for i in range(1, gx - 1, 2) if i + 1 < gx for i, j in ((i, i + 1), (i + 1, i))]
    outer = lax.ppermute(own, "gx", pairs)
    inner = lax.ppermute(own, "gx", between)

    ring_up = [(i, (i + 1) % gz) for i in range(gz)]
    ring_down = [((i + 1) % gz, i) for i in range(gz)]
    up, down, h1, r1, fh, push = call(
        z_faces,
        [f32(Z_UP, *plane), f32(Z_DOWN, *plane), f32(4, 3, *plane), f32(4, 3, *plane)]
        + [f32(4, 2, *plane), f32(4, *plane)],
        (planes, beside, own),
        flops=1_000_000,
        name="z_faces",
    )
    before = lax.ppermute(up, "gz", ring_up)
    after = lax.ppermute(down, "gz", ring_down)
    lows, highs, up, down = call(columns_on, [f32(3, *plane)] * 2 + [f32(72, 128), f32(73, 128)], (own, outer, inner), size=1 << 30, flops=1 << 36, name="columns_on")
    columns_before = lax.ppermute(up, "gz", ring_up)
    columns_after = lax.ppermute(down, "gz", ring_down)

    h1, e1, low = call(
        first_step,
        [f32(5, 3, *plane), f32(6, 3, *plane), f32(2, *plane)],
        (planes, beside, before, after, h1, r1, fh, push),
        flops=1_000_000,
        name="first_step",
    )
    return tuple(
        call(
            second_step,
            [brick] * 4,
            (lows, highs, columns_before, columns_after, h1, e1, low, p1, j1, fh, fe),
            scratch=[pltpu.VMEM((3, 4, 16, 128), jnp.float32)] * 4
            + [pltpu.VMEM((5, 3, ROWS, 128), jnp.float32), pltpu.VMEM((6, 3, ROWS, 128), jnp.float32), pltpu.SemaphoreType.DMA((4,))],
            far_out=True,
            flops=2_000_000,
            name="second_step",
        )
    )


def solution(mesh):
    fields = P(None, "gz", "gy", "gx")
    cells = P("gz", "gy", "gx")
    return jax.shard_map(
        on_device,
        mesh=mesh,
        in_specs=(fields, fields, fields, fields, cells, cells),
        out_specs=(fields, fields, fields, fields),
        check_vma=False,
    )
```

```python
import jax
import jax.numpy as jnp
from jax import lax
from jax.experimental import pallas as pl
from jax.experimental.pallas import tpu as pltpu
from jax.sharding import PartitionSpec as P

time_step = 0.5
damping = 0.2
omega_sq = 1.0
strength = 3.0

DECAY = 1.0 + 0.5 * damping * time_step
HOLD = (1.0 - 0.5 * damping * time_step) / DECAY
PULL = time_step * omega_sq / DECAY
GAIN = PULL * strength

EX, EY, EZ, HX, HY, HZ, QX, QY, QZ, CODE = range(10)
EVERY = tuple(range(10))

Y_UP = [(c, 14) for c in (EY, HX, HZ, CODE)] + [(c, 15) for c in EVERY]
Y_DOWN = [(c, 0) for c in (EX, EY, EZ, HX, HY, HZ, QX, QZ, CODE)]
Z_UP, Z_DOWN = 9, 8

ROWS = 24
SPAN = 32


def up_of(n):
    return [(i, i + 1) for i in range(n - 1)]


def down_of(n):
    return [(i + 1, i) for i in range(n - 1)]


def code_of(material, pml):
    return (1 + 4 * material + pml).astype(jnp.float32)


def y_face(cells, c, row):
    e, h, p, j, material, pml = cells
    if c < HX:
        return e[c, :, row, :]
    if c < QX:
        value = h[c - HX, :, row, :]
        if c == HY or row == 15:
            return value
        other, sign = (EZ, 1.0) if c == HX else (EX, -1.0)
        level = pml[:, row, :]
        loss = jnp.where(level > 2, 0.25, jnp.where(level > 1, 0.1, jnp.where(level > 0, 0.025, 0.0)))
        if row == 0:
            return value - sign * time_step / (1.0 - loss) * e[other, :, 1, :]
        return value + sign * time_step / (1.0 - loss) * e[other, :, 14, :]
    if c < CODE:
        return HOLD * j[c - QX, :, row, :] - PULL * p[c - QX, :, row, :]
    return code_of(material[:, row, :], pml[:, row, :])


def block_class():
    return lax.axis_index("gy") % 4


def load_and_faces(*refs):
    far, near, (down, up, late, mixed), done = refs[:6], refs[6:12], refs[12:16], refs[16]
    copies = [pltpu.make_async_copy(a, b, done.at[i]) for i, (a, b) in enumerate(zip(far, near))]
    for copy in copies:
        copy.start()
    for copy in copies:
        copy.wait()
    is_up = block_class() == 2
    down[...] = jnp.zeros_like(down)
    late[...] = jnp.zeros_like(late)
    for i, (c, row) in enumerate(Y_UP):
        value = y_face(near, c, row)
        at = slice(4 * i, 4 * i + 4)
        up[at, :] = value
        if i < len(Y_DOWN):
            low = y_face(near, *Y_DOWN[i])
            down[at, :] = low
            late[at, :] = low
            value = jnp.where(is_up, value, low)
        mixed[at, :] = value


def joined(after, later, before, rows_after, rows_before):
    rows_after[...] = after[0:40, :] + later[...]
    rows_before[...] = before[...]


def own_value(cells, c, z):
    e, h, p, j, material, pml = cells
    if c < HX:
        return e[c, z]
    if c < QX:
        return h[c - HX, z]
    if c < CODE:
        return HOLD * j[c - QX, z] - PULL * p[c - QX, z]
    return code_of(material[z], pml[z])


def edge_columns(value, g, rows):
    lane = lax.broadcasted_iota(jnp.int32, (rows, 128), 1)
    total = jnp.zeros((rows, 128), jnp.float32)
    for c in range(4 * g, min(4 * g + 4, 10)):
        for z in range(4):
            at = SPAN * (c - 4 * g) + 4 * (z + 2)
            total = jnp.where((lane >= at) & (lane < at + 4), roll(value(c, z), at - 126, 1), total)
    return total


def own_planes(*refs):
    cells, (planes, edges, p1, j1, fe) = refs[:6], refs[6:]
    for z in range(4):
        _, _, keep_e, push_e, metal = factors(own_value(cells, CODE, z))
        for k, f in enumerate((keep_e, push_e, metal)):
            fe[z, k] = f
        for k in range(3):
            flow = own_value(cells, QX + k, z) + GAIN * metal * cells[0][k, z]
            j1[k, z] = flow
            p1[k, z] = cells[2][k, z] + time_step * flow
        for c in EVERY:
            planes[z, c] = own_value(cells, c, z)
    for g in range(3):
        edges[g] = edge_columns(lambda c, z: own_value(cells, c, z), g, 16)


def widen_rows(before, after, last, own, beside, edges):
    low, high = block_class() == 3, block_class() == 2
    beside[...] = jnp.zeros_like(beside)
    for z in range(4):
        for i, (c, row) in enumerate(Y_UP):
            at = slice(4 * i + z, 4 * i + z + 1)
            beside[z, c, row - 8 : row - 7, :] = jnp.where(low, last[at, :], before[at, :])
        for i, (c, row) in enumerate(Y_DOWN):
            at = slice(4 * i + z, 4 * i + z + 1)
            beside[z, c, row : row + 1, :] = jnp.where(high, last[at, :], after[at, :])
    for g in range(3):
        edges[g, 0:16, :] = own[g]
        edges[g, 16:24, :] = edge_columns(lambda c, z: beside[z, c], g, 8)


def widened(planes, beside, z, c):
    return jnp.concatenate([planes[z, c], beside[z, c]])


def z_faces(planes, beside, _, up, down, h1, r1, fh, push):
    wide = [[widened(planes, beside, z, c) for c in EVERY] for z in range(4)]
    for z in range(4):
        e = wide[z][EX : EZ + 1]
        h = wide[z][HX : HZ + 1]
        keep_h, push_h, keep_e, push_e, metal = factors(wide[z][CODE])
        later = [wide[z + 1][EX + k] for k in range(2)] if z < 3 else [0.0, 0.0]
        new = magnetic_new(
            h,
            e,
            {0: y_next(e[0]), 2: y_next(e[2])},
            {0: later[0], 1: later[1]},
            {1: x_next(e[1]), 2: x_next(e[2])},
            keep_h,
            push_h,
        )
        flow = [wide[z][QX + k] + GAIN * metal * e[k] for k in range(3)]
        rest = [keep_e * e[k] - push_e * (metal * flow[k]) for k in range(3)]
        for k in range(3):
            h1[z, k] = new[k]
            r1[z, k] = rest[k]
        fh[z, 0] = keep_h
        fh[z, 1] = push_h
        push[z] = push_e
        if z == 0:
            for i, value in enumerate(new + rest[:2] + [wide[z][CODE]] + e[:2]):
                down[i] = value
        if z == 2:
            up[7] = new[0]
            up[8] = new[1]
        if z == 3:
            for i, value in enumerate(new + rest + [wide[z][CODE]]):
                up[i] = value


def sides(own, outer, inner, g):
    near = (lanes() % 4) < 2
    odd = lax.axis_index("gx") % 2 == 1
    left = jnp.where(odd, outer[g], inner[g])
    right = jnp.where(odd, inner[g], outer[g])
    return jnp.where(near, left, own[g]), jnp.where(near, own[g], right)


def columns_on(own, outer, inner, *outs):
    part = (lanes() % SPAN) // 8
    for g in range(3):
        low, high = sides(own, outer, inner, g)
        up = jnp.where(part == 0, roll(low, -16, 1), roll(high, -8, 1))
        down = jnp.where(part == 2, roll(high, 8, 1), roll(low, 16, 1))
        for out in outs:
            out[ROWS * g : ROWS * (g + 1), :] = jnp.where(part < 2, up, down)


def grid_ends():
    place = lax.axis_index("gz")
    return place == 0, place == lax.axis_size("gz") - 1


def lanes():
    return lax.broadcasted_iota(jnp.int32, (ROWS, 128), 1)


def roll(array, shift, axis):
    shift = shift % array.shape[axis]
    return pltpu.roll(array, shift, axis) if shift else array


def factors(code):
    metal = code > 8.5
    dielec = (code > 4.5) & (code < 8.5)
    inside = code > 0.5
    level = code - jnp.where(metal, 9.0, jnp.where(dielec, 5.0, 1.0))
    loss = jnp.where(level > 2.5, 0.25, jnp.where(level > 1.5, 0.1, jnp.where(level > 0.5, 0.025, 0.0)))
    permit = jnp.where(metal, 1.5, jnp.where(dielec, 2.25, 1.0))
    over_h = jnp.where(inside, 1.0 / (1.0 + loss), 0.0)
    over_e = jnp.where(inside, 1.0 / (permit + loss), 0.0)
    return (
        (1.0 - loss) * over_h,
        time_step * over_h,
        (permit - loss) * over_e,
        time_step * over_e,
        jnp.where(metal, 1.0, 0.0),
    )


def magnetic_new(h, e, ey, ez, ex, keep, push):
    curl = (
        (ey[2] - e[2]) - (ez[1] - e[1]),
        (ez[0] - e[0]) - (ex[2] - e[2]),
        (ex[1] - e[1]) - (ey[0] - e[0]),
    )
    return [None if h[k] is None else keep * h[k] - push * curl[k] for k in range(3)]


def curl_back(h, hy, hz, hx):
    return (
        (h[2] - hy[2]) - (h[1] - hz[1]),
        (h[0] - hz[0]) - (h[2] - hx[2]),
        (h[1] - hx[1]) - (h[0] - hy[0]),
    )


def electric_new(e, h, hy, hz, hx, drag, keep, push):
    curl = curl_back(h, hy, hz, hx)
    return [keep * e[k] + push * (curl[k] - drag[k]) for k in range(3)]


x_next = lambda a: roll(a, -1, 1)
x_back = lambda a: roll(a, 1, 1)
y_next = lambda a: roll(a, -1, 0)
y_back = lambda a: roll(a, 1, 0)


def first_step(planes, beside, before, after, part, r1, fh, push, h1, e1, low):
    first, last = grid_ends()

    def from_below(i):
        return jnp.where(first, 0.0, before[i])

    def from_above(i):
        return jnp.where(last, 0.0, after[i])

    def with_next(h, push_h, x, y):
        return [h[0] + push_h * y, h[1] - push_h * x, h[2]]

    def electric(z, rest, push_e, h, back):
        curl = curl_back(
            h,
            {0: y_back(h[0]), 2: y_back(h[2])},
            {0: back[0], 1: back[1]},
            {1: x_back(h[1]), 2: x_back(h[2])},
        )
        for k, r in enumerate(rest):
            e1[z + 1, k] = r + push_e * curl[k]

    keep_h, push_h, _, push_e, _ = factors(from_below(6))
    low[0] = keep_h
    low[1] = push_h
    h = with_next([from_below(k) for k in range(3)], push_h, widened(planes, beside, 0, EX), widened(planes, beside, 0, EY))
    electric(-1, [from_below(3 + k) for k in range(3)], push_e, h, [from_below(7), from_below(8)])
    for z in range(4):
        for k in range(3):
            h1[z, k] = h[k]
        back, h = h, [part[z, k] for k in range(3)]
        if z == 3:
            h = with_next(h, fh[z, 1], from_above(6), from_above(7))
        electric(z, [r1[z, k] for k in range(3)], push[z], h, back)
    for k in range(3):
        h1[4, k] = h[k]
    _, _, _, push_e, _ = factors(from_above(5))
    electric(4, [from_above(3 + k) for k in range(2)], push_e, [from_above(k) for k in range(3)], h)


def columns(own, outer, inner, before, after):
    first, last = grid_ends()
    lane = lanes()
    part = (lane % SPAN) // 8
    values = []
    for g in range(3):
        low, high = sides(own, outer, inner, g)
        rows = slice(ROWS * g, ROWS * (g + 1))
        up = jnp.where(first, 0.0, before[rows, :])
        down = jnp.where(last, 0.0, after[rows, :])
        low = jnp.where(part == 0, up, jnp.where(part == 3, down, low))
        high = jnp.where(part == 0, roll(up, -8, 1), jnp.where(part == 3, roll(down, 8, 1), high))
        for k in range(4):
            values.append(jnp.where(lane < SPAN, roll(low, -SPAN * k, 1), roll(high, SPAN - SPAN * k, 1)))
    z_next = lambda a: roll(a, -4, 1)
    z_back = lambda a: roll(a, 4, 1)

    def shifted(f, y, z, x):
        return {0: y(f[0]), 2: y(f[2])}, {0: z(f[0]), 1: z(f[1])}, {1: x(f[1]), 2: x(f[2])}

    keep_h, push_h, keep_e, push_e, metal = factors(values[CODE])
    e0 = values[EX : EZ + 1]
    h1 = magnetic_new(values[HX : HZ + 1], e0, *shifted(e0, y_next, z_next, x_next), keep_h, push_h)
    drag = [metal * (values[QX + k] + GAIN * e0[k]) for k in range(3)]
    e1 = electric_new(e0, h1, *shifted(h1, y_back, z_back, x_back), drag, keep_e, push_e)
    h2 = magnetic_new(h1, e1, *shifted(e1, y_next, z_next, x_next), keep_h, push_h)
    return h1, e1, h2


def second_step(own, outer, inner, before, after, h1, e1, low, p1, j1, fh, fe, *rest):
    outs, near, h2, fixed, done = rest[:4], rest[4:8], rest[8], rest[9], rest[10]
    e_near, h_near, p_near, j_near = near
    lane = lanes()
    ch1, ce1, ch2 = columns(own, outer, inner, before, after)

    def at_ends(column):
        return jnp.where(lane % 4 == 1, roll(column, -SPAN, 1), column)

    def put_right(array, z, column):
        return jnp.where((lane == 0) | (lane == 127), roll(column, 127 - (4 * (z + 2) + 1), 1), array)

    ends_h = [at_ends(a) for a in ch1]
    ends_e = [at_ends(a) for a in ce1]

    def after_x(array, z):
        return lambda k: jnp.where(lane == 127, roll(ce1[k], 127 - (SPAN + 4 * (z + 2) + 2), 1), x_next(array[k]))

    def before_x(array, z):
        return lambda k: jnp.where(lane == 0, roll(ch2[k], -(4 * (z + 2) + 1), 1), x_back(array[k]))

    def fixed_e(z):
        return [put_right(e1[z + 1, k], z, ends_e[k]) for k in range(3 if z < 4 else 2)]

    for z in range(-1, 5):
        for k, a in enumerate(fixed_e(z)):
            fixed[z + 1, k] = a
    copies = [pltpu.make_async_copy(a, b, done.at[i]) for i, (a, b) in enumerate(zip(near, outs))]
    for z in range(4):
        metal = fe[z, 2]
        for k in range(3):
            e = fixed[z + 1, k, 0:16, :]
            flow = HOLD * j1[k, z] - PULL * p1[k, z] + GAIN * metal * e
            j_near[k, z] = flow
            p_near[k, z] = p1[k, z] + time_step * flow
    copies[2].start()
    copies[3].start()
    e = [fixed[0, k] for k in range(3)]
    for z in range(-1, 4):
        up = [fixed[z + 2, k] for k in range(3 if z < 3 else 2)]
        h = [h1[z + 1, 0]] + [put_right(h1[z + 1, k], z, ends_h[k]) for k in (1, 2)]
        x = after_x(e, z)
        new = magnetic_new(
            h,
            e,
            {0: y_next(e[0]), 2: y_next(e[2])},
            {0: up[0], 1: up[1]},
            {1: x(1), 2: x(2)},
            fh[z, 0] if z >= 0 else low[0],
            fh[z, 1] if z >= 0 else low[1],
        )
        for k in range(3):
            h2[z + 1, k] = new[k]
            if z >= 0:
                h_near[k, z] = new[k][0:16]
        e = up
    copies[1].start()
    for z in range(4):
        h = [h2[z + 1, k] for k in range(3)]
        down = [h2[z, k] for k in range(2)]
        x = before_x(h, z)
        new = electric_new(
            [fixed[z + 1, k, 0:16, :] for k in range(3)],
            [a[0:16] for a in h],
            {0: y_back(h[0])[0:16], 2: y_back(h[2])[0:16]},
            {0: down[0][0:16], 1: down[1][0:16]},
            {1: x(1)[0:16], 2: x(2)[0:16]},
            [fe[z, 2] * j_near[k, z] for k in range(3)],
            fe[z, 0],
            fe[z, 1],
        )
        for k in range(3):
            e_near[k, z] = new[k]
    copies[0].start()
    for copy in copies:
        copy.wait()


VMEM = pl.BlockSpec(memory_space=pltpu.VMEM)
HBM = pl.BlockSpec(memory_space=pltpu.HBM)


def call(kernel, outs, args, scratch=(), flops=0, size=0, far=False, far_out=False, name=None):
    size = size or sum(a.size for a in args) + sum(o.size for o in outs)
    return pl.pallas_call(
        kernel,
        out_shape=outs,
        in_specs=[HBM if far else VMEM] * len(args),
        out_specs=[HBM if far_out else VMEM] * len(outs),
        scratch_shapes=list(scratch),
        cost_estimate=pl.CostEstimate(flops=flops, bytes_accessed=4 * size, transcendentals=0),
        compiler_params=pltpu.CompilerParams(vmem_limit_bytes=16 * 2**20),
        name=name,
    )(*args)


def f32(*shape):
    return jax.ShapeDtypeStruct(shape, jnp.float32)


def on_device(electric, magnetic, polar, current, material, pml):
    cells = (electric, magnetic, polar, current, material, pml)
    gx, gy, gz = (lax.axis_size(a) for a in ("gx", "gy", "gz"))
    shapes = [jax.ShapeDtypeStruct(a.shape, a.dtype) for a in cells]
    cells = [pltpu.with_memory_space_constraint(a, pltpu.HBM) for a in cells]
    *cells, down, up, late, mixed = call(
        load_and_faces,
        [*shapes, f32(64, 128), f32(56, 128), f32(40, 128), f32(56, 128)],
        cells,
        scratch=[pltpu.SemaphoreType.DMA((6,))],
        far=True,
        name="load_and_faces",
    )
    ups, downs = up_of(gy), down_of(gy)
    after = lax.ppermute(down, "gy", [(i, j) for i, j in downs if i % 4 in (1, 2)])
    before = lax.ppermute(up, "gy", [(i, j) for i, j in ups if i % 4 != 2])
    later = lax.ppermute(late, "gy", [(i, j) for i, j in downs if i % 4 == 0])
    last = lax.ppermute(mixed, "gy", [(i, j) for i, j in ups if i % 4 == 2] + [(i, j) for i, j in downs if i % 4 == 3])
    after, before = call(
        joined,
        [f32(40, 128), f32(56, 128)],
        (after, later, before),
        size=1 << 30,
        flops=1 << 36,
        name="joined",
    )
    brick, plane = f32(3, 4, 16, 128), (ROWS, 128)
    planes, own, p1, j1, fe = call(
        own_planes,
        [f32(4, 10, 16, 128), f32(3, 16, 128), brick, brick, f32(4, 3, 16, 128)],
        cells,
        name="own_planes",
    )
    beside, own = call(
        widen_rows,
        [f32(4, 10, 8, 128), f32(3, *plane)],
        (before, after, last, own),
        name="widen_rows",
    )
    pairs = [(i, i ^ 1) for i in range(gx) if i ^ 1 < gx]
    between = [(i, j) for i in range(1, gx - 1, 2) if i + 1 < gx for i, j in ((i, i + 1), (i + 1, i))]
    outer = lax.ppermute(own, "gx", pairs)
    inner = lax.ppermute(own, "gx", between)

    ring_up = [(i, (i + 1) % gz) for i in range(gz)]
    ring_down = [((i + 1) % gz, i) for i in range(gz)]
    up, down, h1, r1, fh, push = call(
        z_faces,
        [f32(Z_UP, *plane), f32(Z_DOWN, *plane), f32(4, 3, *plane), f32(4, 3, *plane)]
        + [f32(4, 2, *plane), f32(4, *plane)],
        (planes, beside, own),
        flops=1_000_000,
        name="z_faces",
    )
    before = lax.ppermute(up, "gz", ring_up)
    after = lax.ppermute(down, "gz", ring_down)
    up, down = call(columns_on, [f32(72, 128), f32(73, 128)], (own, outer, inner), size=1 << 30, flops=1 << 36, name="columns_on")
    columns_before = lax.ppermute(up, "gz", ring_up)
    columns_after = lax.ppermute(down, "gz", ring_down)

    h1, e1, low = call(
        first_step,
        [f32(5, 3, *plane), f32(6, 3, *plane), f32(2, *plane)],
        (planes, beside, before, after, h1, r1, fh, push),
        flops=1_000_000,
        name="first_step",
    )
    return tuple(
        call(
            second_step,
            [brick] * 4,
            (own, outer, inner, columns_before, columns_after, h1, e1, low, p1, j1, fh, fe),
            scratch=[pltpu.VMEM((3, 4, 16, 128), jnp.float32)] * 4
            + [pltpu.VMEM((5, 3, ROWS, 128), jnp.float32), pltpu.VMEM((6, 3, ROWS, 128), jnp.float32), pltpu.SemaphoreType.DMA((4,))],
            far_out=True,
            flops=2_000_000,
            name="second_step",
        )
    )


def solution(mesh):
    fields = P(None, "gz", "gy", "gx")
    cells = P("gz", "gy", "gx")
    return jax.shard_map(
        on_device,
        mesh=mesh,
        in_specs=(fields, fields, fields, fields, cells, cells),
        out_specs=(fields, fields, fields, fields),
        check_vma=False,
    )
```
